128 devices in a mesh: dp: 4 (over y), tensor: 32 (over x, z, core).
Axes of the slice: x: 4, y: 4, z: 4, core: 2. Of those that a mesh axis runs over, the one named last changes fastest.
Arguments:
- tokens_in: bfloat16 [3072, 5120], P('dp', 'tensor')
- out_grad: bfloat16 [3072, 5120], P('dp', 'tensor'), may hold values from -6 to 6
- tenant: int32 [3072], P('dp'), may hold values from 0 to 32767, as said below
- slot_of: int32 [32768], replicated, may hold values from 0 to 32767, as said below
- steer_table: bfloat16 [32768, 5120], P(('dp', 'tensor')), may hold values from -6 to 6
- norm_gain: bfloat16 [5120], P('tensor'), may hold values from 0.099609375 to 1.8984375
- w_gate: bfloat16 [5120, 16384], P(None, 'tensor'), may hold values from -0.078125 to 0.078125
- w_up: bfloat16 [5120, 16384], P(None, 'tensor'), may hold values from -0.078125 to 0.078125
- w_down: bfloat16 [16384, 5120], P('tensor'), may hold values from -0.046875 to 0.046875
Outputs:
- input_grad: bfloat16 [3072, 5120], P('dp', 'tensor')
- table_grad: float32 [32768, 5120], P(('dp', 'tensor'))
The draws below stay inside these ranges and needn't reach their ends.
Inputs may be any that keep to these rules, and one draw needn't show every extreme that they name: slot_of names every row of the table exactly once. `tenant`: in each aligned block of 768 tokens (one dp index), at most 24 tokens have tenants t with slot_of[t] // 256 equal to one value, and in every block some value is taken by exactly 24 tokens.
All inputs are finite; a program needn't handle non-finite values.
Results may differ from the reference program's by a relative error of at most 0.0065.
Values may be sent and summed in bfloat16 or wider, within the bound.
A program may use at most 128 MiB of HBM per device.

```python
import math
import jax
import jax.numpy as jnp
from jax import lax

D = 5120
FF = 16384
TOK_DEV = 768
TEN_DEV = 256
TOKENS = 3072
TENANTS = 32768
N_DP = 4


def slot_table(key):
    return jax.random.permutation(jax.random.fold_in(key, 7), TENANTS).astype(jnp.int32)


def draw_slot_of(key, part):
    shared = slot_table(key)
    return shared


def force_hot(order, hottest):
    where_hot = jnp.argmax(order == hottest)
    order = order.at[where_hot].set(order[3])
    return order.at[3].set(hottest)


def draw_tenant(key, part):
    shared = slot_table(key)
    key = jax.random.fold_in(key, 5)
    inverse = jnp.argsort(shared).astype(jnp.int32)
    holders = TENANTS // TEN_DEV
    quads = holders // 4
    share = 4 * TOK_DEV // holders
    subkeys = jax.random.split(key, 6)
    cuts = jnp.sort(jax.random.randint(subkeys[0], (N_DP, quads, 3), 0, share + 1), axis=2)
    cuts = cuts.at[:, 0, :].set(0)
    edges = jnp.concatenate([jnp.zeros((N_DP, quads, 1), jnp.int32), cuts.astype(jnp.int32), jnp.full((N_DP, quads, 1), share, jnp.int32)], axis=2)
    counts = (edges[:, :, 1:] - edges[:, :, :-1]).reshape(N_DP, holders)
    ends = jnp.cumsum(counts, axis=1)
    position = jnp.arange(TOK_DEV, dtype=jnp.int32)
    which = jax.vmap(lambda bounds: jnp.searchsorted(bounds, position, side='right'))(ends).astype(jnp.int32)
    orders = jax.vmap(lambda sub: jax.random.permutation(sub, holders))(jax.random.split(subkeys[1], N_DP)).astype(jnp.int32)
    hottest = jax.random.randint(subkeys[2], (), 0, holders).astype(jnp.int32)
    orders = jax.vmap(lambda order: force_hot(order, hottest))(orders)
    owners = jnp.take_along_axis(orders, which, axis=1)
    shuffles = jax.vmap(lambda sub: jax.random.permutation(sub, TOK_DEV))(jax.random.split(subkeys[3], N_DP)).astype(jnp.int32)
    owners = jnp.take_along_axis(owners, shuffles, axis=1)
    first = jax.random.randint(subkeys[4], (N_DP, TOK_DEV), 0, TEN_DEV)
    second = jax.random.randint(subkeys[5], (N_DP, TOK_DEV), 0, TEN_DEV)
    local_row = first * second // TEN_DEV
    return inverse[owners * TEN_DEV + local_row].reshape(TOKENS).astype(jnp.int32)


def draw_tokens_in(key, part):
    key = jax.random.fold_in(key, 11)
    ramp = jnp.exp(math.log(3.0) * jnp.arange(D, dtype=jnp.float32) / (D - 1))
    values = jax.random.normal(key, (TOKENS, D), jnp.float32) * ramp * 0.6
    return values.astype(jnp.bfloat16)


def level_of(key, shape, pieces, smallest, largest):
    def one(axis_at, blocks):
        draws = jax.random.uniform(jax.random.fold_in(jax.random.fold_in(key, 6), axis_at), (blocks,), jnp.float32, smallest / len(pieces), largest / len(pieces))
        return jnp.repeat(jnp.exp(draws), shape[axis_at] // blocks).reshape((-1,) + (1,) * (len(shape) - axis_at - 1))

    gain = one(*pieces[0])
    for cut in pieces[1:]:
        gain = gain * one(*cut)
    return gain


def gaussian(key, extent, deviation, limit, cuts=(), held_as=jnp.bfloat16):
    values = jax.random.normal(key, extent, jnp.float32) * deviation
    if len(cuts) > 0:
        values = level_of(key, extent, cuts, -0.22, 0.18) * values
    return jnp.clip(values, min=-limit, max=limit).astype(held_as)


def setup_inputs(seed: int = 0) -> dict:
    arg_keys = jax.random.split(jax.random.key(seed), 10)
    return {
        "tokens_in": draw_tokens_in(jax.random.fold_in(arg_keys[9], 71), 0),
        "out_grad": gaussian(arg_keys[1], (TOKENS, D), 1.0, 6.0, ((0, 4), (1, 32))),
        "tenant": draw_tenant(jax.random.fold_in(arg_keys[9], 71), 0),
        "slot_of": draw_slot_of(jax.random.fold_in(arg_keys[9], 71), 0),
        "steer_table": gaussian(arg_keys[4], (TENANTS, D), 1.0, 6.0, ((0, 128),)),
        "norm_gain": jnp.clip(1.0 + 0.18 * jax.random.normal(arg_keys[5], (D,), jnp.float32), 0.099609375, 1.8984375).astype(jnp.bfloat16),
        "w_gate": gaussian(arg_keys[6], (D, FF), D ** -0.5, 0.078125, ((1, 32),)),
        "w_up": gaussian(arg_keys[7], (D, FF), D ** -0.5, 0.078125, ((1, 32),)),
        "w_down": gaussian(arg_keys[8], (FF, D), FF ** -0.5, 0.046875, ((0, 32),)),
    }


def silu_parts(values):
    sigma = jax.nn.sigmoid(values)
    return (values * sigma, sigma * (1.0 + values * (1.0 - sigma)))

def reference(tokens_in, out_grad, tenant, slot_of, steer_table, norm_gain, w_gate, w_up, w_down):
    table_slot = slot_of[tenant].astype(jnp.int32)
    steering = steer_table[table_slot]
    residual = (tokens_in.astype(jnp.float32) + steering.astype(jnp.float32)).astype(jnp.bfloat16)
    residual_wide = residual.astype(jnp.float32)
    inverse_rms = lax.rsqrt(lax.optimization_barrier(jnp.mean(residual_wide * residual_wide, axis=1, keepdims=True)) + 1e-06)
    gain_wide = norm_gain.astype(jnp.float32)
    normed = (residual_wide * inverse_rms * gain_wide).astype(jnp.bfloat16)
    gate_out = jnp.dot(normed, w_gate, preferred_element_type=jnp.float32)
    up_out = jnp.dot(normed, w_up, preferred_element_type=jnp.float32)
    contract = (((1,), (1,)), ((), ()))
    hidden_grad = lax.dot_general(out_grad, w_down, contract, preferred_element_type=jnp.float32)
    activated, derivative = silu_parts(gate_out)
    gate_grad = (hidden_grad * up_out * derivative).astype(jnp.bfloat16)
    up_grad = (hidden_grad * activated).astype(jnp.bfloat16)
    norm_grad = lax.dot_general(gate_grad, w_gate, contract, preferred_element_type=jnp.float32)
    norm_grad = norm_grad + lax.dot_general(up_grad, w_up, contract, preferred_element_type=jnp.float32)
    row_dot = lax.optimization_barrier(jnp.sum(norm_grad * gain_wide * residual_wide, axis=1, keepdims=True))
    full_grad = out_grad.astype(jnp.float32) + gain_wide * inverse_rms * norm_grad
    full_grad = full_grad - residual_wide * inverse_rms ** 3 * row_dot / D
    table_grad = jax.ops.segment_sum(full_grad, table_slot, num_segments=TENANTS)
    return (full_grad.astype(jnp.bfloat16), table_grad)
```

```python
import jax
import jax.numpy as jnp
from jax import lax
from jax.sharding import PartitionSpec as P

D = 5120
F32 = jnp.float32
BF16 = jnp.bfloat16


def silu_parts(values):
    sigma = jax.nn.sigmoid(values)
    return (values * sigma, sigma * (1.0 + values * (1.0 - sigma)))


def dot(a, b, ca, cb):
    return lax.dot_general(a, b, (((ca,), (cb,)), ((), ())), preferred_element_type=F32)


def one_hot(index, size):
    return index[..., None] == jnp.arange(size, dtype=jnp.int32)


def look_up_slots(slot_of, tenant):
    lines = slot_of.reshape(-1, 128)
    halves = jnp.concatenate([lines // 256, lines % 256], axis=1).astype(BF16)
    picked = dot(one_hot(tenant // 128, lines.shape[0]).astype(BF16), halves, 1, 0)
    lane = one_hot(tenant % 128, 128)
    owners = jnp.sum(jnp.where(lane, picked[:, :128], 0.0), axis=1).astype(jnp.int32)
    rows = jnp.sum(jnp.where(lane, picked[:, 128:], 0.0), axis=1).astype(jnp.int32)
    return owners, rows


def per_device(tokens_in, out_grad, tenant, slot_of, steer_table, norm_gain, w_gate, w_up, w_down):
    holders = lax.axis_size(("dp", "tensor"))
    groups = lax.axis_size("dp")
    width_parts = lax.axis_size("tensor")
    rows_own = steer_table.shape[0]
    feat_local = tokens_in.shape[1]
    token_count = tenant.shape[0]
    capacity = 4 * token_count // holders
    group = lax.axis_index("dp")
    me = lax.axis_index(("dp", "tensor"))

    tenant_all = lax.all_gather(tenant, "dp", axis=0, tiled=True)
    out_grad_t = out_grad.T
    out_grad_full = lax.all_gather(out_grad_t, "tensor", axis=0, tiled=True)
    gain_padded = jnp.pad(norm_gain[None, :], ((0, 15), (0, 96)))
    gain_full = lax.all_gather(gain_padded, "tensor", axis=0, tiled=False)[:, 0, :feat_local].reshape(-1, 1).astype(F32)

    owners_all, rows_all = look_up_slots(slot_of, tenant_all)
    earlier = (
        jnp.arange(token_count, dtype=jnp.int32)[:, None] < jnp.arange(token_count, dtype=jnp.int32)[None, :]
    ).astype(BF16)
    mine = (owners_all == me).reshape(groups, token_count)
    rank_mine = dot(mine.astype(BF16), earlier, 1, 0).astype(jnp.int32)
    slot_of_token = jnp.where(mine, rank_mine, -1)
    slots = (slot_of_token[:, None, :] == jnp.arange(capacity, dtype=jnp.int32)[None, :, None]).astype(BF16)
    row_hot = one_hot(rows_all.reshape(groups, token_count), rows_own).astype(BF16)
    wanted = lax.dot_general(slots, row_hot, (((2,), (1,)), ((0,), (0,))), preferred_element_type=F32)
    wanted = wanted.astype(BF16).reshape(groups * capacity, rows_own)
    picked = dot(wanted, steer_table, 1, 0).astype(BF16)
    outgoing = picked.reshape(groups, capacity, width_parts, feat_local).transpose(0, 2, 1, 3)
    outgoing = outgoing.reshape(holders, capacity, feat_local)
    returned = lax.all_to_all(outgoing, ("dp", "tensor"), split_axis=0, concat_axis=0, tiled=True)
    returned = returned.reshape(holders * capacity, feat_local)

    owners = lax.dynamic_slice_in_dim(owners_all, group * token_count, token_count)
    matches = one_hot(owners, holders).astype(BF16)
    before = dot(earlier, matches, 0, 0)
    ranking = jnp.sum(jnp.where(matches > 0, before, 0.0), axis=1).astype(jnp.int32)
    place = one_hot(owners * capacity + ranking, holders * capacity).astype(BF16)
    steering = dot(returned, place, 0, 1)

    residual = (tokens_in.T.astype(F32) + steering).astype(BF16)
    residual_full = lax.all_gather(residual, "tensor", axis=0, tiled=True).astype(F32)
    inverse_rms = lax.rsqrt(jnp.sum(residual_full * residual_full, axis=0, keepdims=True) / D + 1e-06)
    normed = (residual_full * inverse_rms * gain_full).astype(BF16)
    hidden_grad = dot(w_down, out_grad_full, 1, 0)
    gate_out = dot(w_gate, normed, 0, 0)
    up_out = dot(w_up, normed, 0, 0)
    activated, derivative = silu_parts(gate_out)
    gate_grad = (hidden_grad * up_out * derivative).astype(BF16)
    up_grad = (hidden_grad * activated).astype(BF16)
    dot_part = jnp.sum(gate_grad.astype(F32) * gate_out + up_grad.astype(F32) * up_out, axis=0)
    dot_parts = lax.all_gather(dot_part, "tensor", axis=0, tiled=False)
    term = dot(w_gate, gate_grad, 1, 0) + dot(w_up, up_grad, 1, 0)
    norm_grad = lax.psum_scatter(term.astype(BF16), "tensor", scatter_dimension=0, tiled=True).astype(F32)
    row_dot = jnp.sum(dot_parts, axis=0, keepdims=True) / inverse_rms
    gain_wide = norm_gain.astype(F32)[:, None]
    residual_wide = residual.astype(F32)
    full_grad = out_grad_t.astype(F32) + gain_wide * inverse_rms * norm_grad
    full_grad = (full_grad - residual_wide * inverse_rms**3 * row_dot / D).astype(BF16)

    sending = dot(place, full_grad, 0, 1).astype(BF16).reshape(holders, capacity, feat_local)
    received = lax.all_to_all(sending, ("dp", "tensor"), split_axis=0, concat_axis=0, tiled=True)
    received = received.reshape(groups, width_parts, capacity, feat_local).transpose(0, 2, 1, 3)
    received = received.reshape(groups * capacity, width_parts * feat_local)
    table_grad = dot(wanted, received, 0, 0)
    return (full_grad.T, table_grad)


def solution(mesh):
    placed = (
        P("dp", "tensor"),
        P("dp", "tensor"),
        P("dp"),
        P(),
        P(("dp", "tensor"), None),
        P("tensor"),
        P(None, "tensor"),
        P(None, "tensor"),
        P("tensor", None),
    )
    return jax.shard_map(
        per_device,
        mesh=mesh,
        in_specs=placed,
        out_specs=(P("dp", "tensor"), P(("dp", "tensor"), None)),
        check_vma=False,
    )
```

```python
import functools

import jax
import jax.numpy as jnp
from jax import lax
from jax.experimental import pallas as pl
from jax.experimental.pallas import tpu as pltpu
from jax.sharding import PartitionSpec as P

D = 5120
F32 = jnp.float32
BF16 = jnp.bfloat16


def dot(a, b, ca, cb):
    return lax.dot_general(a, b, (((ca,), (cb,)), ((), ())), preferred_element_type=F32)


def one_hot(index, size):
    return index[..., None] == jnp.arange(size, dtype=jnp.int32)


def look_up_slots(slot_of, tenant):
    lines = slot_of.reshape(-1, 128)
    halves = jnp.concatenate([lines // 256, lines % 256], axis=1).astype(BF16)
    picked = dot(one_hot(tenant // 128, lines.shape[0]).astype(BF16), halves, 1, 0)
    lane = one_hot(tenant % 128, 128)
    owners = jnp.sum(jnp.where(lane, picked[:, :128], 0.0), axis=1).astype(jnp.int32)
    rows = jnp.sum(jnp.where(lane, picked[:, 128:], 0.0), axis=1).astype(jnp.int32)
    return owners, rows


CHUNKS = 3
SIDE = 4
HALF = 80
KB = 640
AG_P1 = 0
AG_P2 = 6
AG_SIB = 12
RS_SIB = 20
RS_R1 = 24
RS_R2 = 30
DOT_SIB = 36
DOT_X = 37
DOT_Z = 40
SLOTS = 43


def core_kernel(
    res_ref, og_own_ref, gain_own_ref, og_hbm, wd_hbm, wg_hbm, wu_hbm, wgt_hbm, wut_hbm,
    out_ref,
    x_all, wg, wu, wgt, wut, gain, og_buf, wd_buf, hid, y_buf, g_acc, u_acc, both, inv_s,
    part, sib_in, ra, rb, rc, rst, rsum, qa, qb, qc, qst,
    dp_, ds, dq, dxf, dxb, dxo, dr, dzf, dzb, dzo,
    ssem, rsem, lsem, hsem,
):
    ten = lax.axis_index("tensor")
    x = ten // 8
    z = lax.rem(ten // 2, 4)
    c = lax.rem(ten, 2)
    step = 1 - 2 * c
    xf, xb, xo = lax.rem(x + step + 4, 4), lax.rem(x - step + 4, 4), lax.rem(x + 2, 4)
    zf, zb, zo = lax.rem(z + step + 4, 4), lax.rem(z - step + 4, 4), lax.rem(z + 2, 4)

    def dev(xx, zz, cc):
        return {"tensor": (xx * 4 + zz) * 2 + cc}

    to_xf, to_xb = dev(xf, z, c), dev(xb, z, c)
    to_zf, to_zb = dev(x, zf, c), dev(x, zb, c)
    to_sib = dev(x, z, 1 - c)
    width = res_ref.shape[1]
    tok = width // CHUNKS
    rows = SIDE * 2 * 2 * HALF

    local = [
        pltpu.make_async_copy(wgt_hbm, wgt, lsem.at[0]),
        pltpu.make_async_copy(wut_hbm, wut, lsem.at[1]),
        pltpu.make_async_copy(wg_hbm, wg, lsem.at[2]),
        pltpu.make_async_copy(wu_hbm, wu, lsem.at[3]),
        pltpu.make_async_copy(og_hbm.at[:, pl.ds(width, 128)], gain, lsem.at[4]),
    ]

    def hidden_copies(j):
        return (
            pltpu.make_async_copy(og_hbm.at[pl.ds(j * KB, KB), pl.ds(0, width)], og_buf.at[j % 2], hsem.at[0, j % 2]),
            pltpu.make_async_copy(wd_hbm.at[:, pl.ds(j * KB, KB)], wd_buf.at[j % 2], hsem.at[1, j % 2]),
        )

    for copy in hidden_copies(0) + hidden_copies(1):
        copy.start()
    for copy in local:
        copy.start()

    for k in range(CHUNKS):
        for h in range(2):
            x_all[k, x, z, c, h] = res_ref[h * HALF:(h + 1) * HALF, k * tok:(k + 1) * tok]

    barrier = pltpu.get_barrier_semaphore()
    for where in (to_xf, to_xb, to_zf, to_zb, to_sib):
        pl.semaphore_signal(barrier, inc=1, device_id=where, device_id_type=pl.DeviceIdType.MESH)
    pl.semaphore_wait(barrier, 5)

    sent = []

    def move(src, dst, k, slot, where):
        copy = pltpu.make_async_remote_copy(
            src_ref=src, dst_ref=dst, send_sem=ssem.at[k, slot], recv_sem=rsem.at[k, slot],
            device_id=where, device_id_type=pl.DeviceIdType.MESH,
        )
        copy.start()
        sent.append(copy)

    def arrived(dst, k, slot, where):
        pltpu.make_async_remote_copy(
            src_ref=dst, dst_ref=dst, send_sem=ssem.at[k, slot], recv_sem=rsem.at[k, slot],
            device_id=where, device_id_type=pl.DeviceIdType.MESH,
        ).wait_recv()

    def one(k, xx, zz, h):
        return x_all.at[k, xx, zz, c, h]

    def line(k, h, at, cc):
        return x_all.at[k, at, :, cc, 0] if h == 0 else x_all.at[k, :, at, cc, 1]

    near_to = ((to_zf, to_zb), (to_xf, to_xb))
    far_to = ((to_xf, to_xb), (to_zf, to_zb))
    far_at = ((x, xb, xf, xo), (z, zb, zf, zo))

    def near(k, h, at):
        return one(k, x, at, 0) if h == 0 else one(k, at, z, 1)

    near_at = ((z, zb, zf, zo), (x, xb, xf, xo))

    def ag1(k):
        for h in range(2):
            own = one(k, x, z, h)
            move(own, own, k, AG_P1 + 3 * h, near_to[h][0])
            move(own, own, k, AG_P1 + 3 * h + 1, near_to[h][1])

    def ag2(k):
        for h in range(2):
            behind = near(k, h, near_at[h][1])
            arrived(behind, k, AG_P1 + 3 * h, near_to[h][1])
            move(behind, behind, k, AG_P1 + 3 * h + 2, near_to[h][0])

    def ag3(k):
        for h in range(2):
            arrived(near(k, h, near_at[h][2]), k, AG_P1 + 3 * h + 1, near_to[h][0])
            arrived(near(k, h, near_at[h][3]), k, AG_P1 + 3 * h + 2, near_to[h][1])
            own = line(k, h, far_at[h][0], c)
            move(own, own, k, AG_P2 + 3 * h, far_to[h][0])
            move(own, own, k, AG_P2 + 3 * h + 1, far_to[h][1])
            move(own, own, k, AG_SIB + 4 * h, to_sib)

    def ag4(k):
        for h in range(2):
            behind = line(k, h, far_at[h][1], c)
            arrived(behind, k, AG_P2 + 3 * h, far_to[h][1])
            move(behind, behind, k, AG_P2 + 3 * h + 2, far_to[h][0])
            move(behind, behind, k, AG_SIB + 4 * h + 1, to_sib)
        for h in range(2):
            ahead = line(k, h, far_at[h][2], c)
            arrived(ahead, k, AG_P2 + 3 * h + 1, far_to[h][0])
            move(ahead, ahead, k, AG_SIB + 4 * h + 2, to_sib)

    def ag5(k):
        for h in range(2):
            opposite = line(k, h, far_at[h][3], c)
            arrived(opposite, k, AG_P2 + 3 * h + 2, far_to[h][1])
            move(opposite, opposite, k, AG_SIB + 4 * h + 3, to_sib)

    def ag6(k):
        for h in range(2):
            at = far_at[h]
            for n, i in enumerate((0, 2, 1, 3)):
                arrived(line(k, h, at[i], 1 - c), k, AG_SIB + 4 * h + n, to_sib)

    def hidden(j):
        for copy in hidden_copies(j):
            copy.wait()
        part_sum = jnp.dot(wd_buf[j % 2], og_buf[j % 2], preferred_element_type=F32)
        if j == 0:
            hid[...] = part_sum
        else:
            hid[...] += part_sum
        if j + 2 < D // KB:
            for copy in hidden_copies(j + 2):
                copy.start()

    def gates(k):
        g_acc[...] = jnp.zeros_like(g_acc)
        u_acc[...] = jnp.zeros_like(u_acc)

        def body(i, squares):
            at = pl.multiple_of(i * rows, rows)
            wide = x_all[k, i].reshape(rows, tok).astype(F32)
            scale = gain[pl.ds(at, rows), :].astype(F32)
            scale = jnp.concatenate([scale] * (tok // 128), axis=1)
            y_buf[...] = (wide * scale).astype(BF16)
            g_acc[...] += jnp.dot(wgt[:, pl.ds(at, rows)], y_buf[...], preferred_element_type=F32)
            u_acc[...] += jnp.dot(wut[:, pl.ds(at, rows)], y_buf[...], preferred_element_type=F32)
            return squares + jnp.sum(wide * wide, axis=0, keepdims=True)

        squares = lax.fori_loop(0, SIDE, body, jnp.zeros((1, tok), F32))
        inverse = lax.rsqrt(squares / D + 1e-06)
        inv_s[k] = jnp.broadcast_to(inverse, (8, tok))
        gate_out = g_acc[...] * inverse
        up_out = u_acc[...] * inverse
        hidden_grad = hid[:, k * tok:(k + 1) * tok]
        sigma = jax.nn.sigmoid(gate_out)
        gate_grad = (hidden_grad * up_out * (sigma * (1.0 + gate_out * (1.0 - sigma)))).astype(BF16)
        up_grad = (hidden_grad * (gate_out * sigma)).astype(BF16)
        half = gate_grad.shape[0]
        both[0:half] = gate_grad
        both[half:2 * half] = up_grad
        dots = jnp.sum(gate_grad.astype(F32) * gate_out + up_grad.astype(F32) * up_out, axis=0, keepdims=True)
        dp_[k] = jnp.broadcast_to(dots, (8, tok))
        move(dp_.at[k], dq.at[k], k, DOT_SIB, to_sib)

    def last(k):
        half = both.shape[0] // 2

        for i in range(SIDE):
            at = i * rows
            term = jnp.dot(wg[at:at + rows, :], both[0:half], preferred_element_type=F32)
            term = term + jnp.dot(wu[at:at + rows, :], both[half:2 * half], preferred_element_type=F32)
            part[k, i] = term.astype(BF16).reshape(SIDE, 2, 2, HALF, tok)
            move(part.at[k, i, :, 1 - c], sib_in.at[k, i], k, RS_SIB + i, to_sib)

    def add(*refs_):
        total = refs_[0].astype(F32)
        for other in refs_[1:]:
            total = total + other.astype(F32)
        return total

    def chip_line(k, h, at):
        return part.at[k, at, :, c, 0] if h == 0 else part.at[k, :, at, c, 1]

    def rs0(k):
        for i in range(SIDE):
            arrived(sib_in.at[k, i], k, RS_SIB + i, to_sib)
            part[k, i, :, c] = add(part[k, i, :, c], sib_in[k, i]).astype(BF16)
        for h in range(2):
            move(chip_line(k, h, far_at[h][3]), ra.at[k, h], k, RS_R1 + 3 * h, far_to[h][0])
        for h in range(2):
            move(chip_line(k, h, far_at[h][1]), rb.at[k, h], k, RS_R1 + 3 * h + 1, far_to[h][1])
        arrived(dq.at[k], k, DOT_SIB, to_sib)
        ds[k] = dp_[k] + dq[k]

    def rs0b(k):
        move(ds.at[k], dxf.at[k], k, DOT_X, to_xf)
        move(ds.at[k], dxb.at[k], k, DOT_X + 1, to_xb)

    def rs1(k):
        for h in range(2):
            arrived(ra.at[k, h], k, RS_R1 + 3 * h, far_to[h][1])
            rst[k, h] = add(ra[k, h], chip_line(k, h, far_at[h][2])[...]).astype(BF16)
            move(rst.at[k, h], rc.at[k, h], k, RS_R1 + 3 * h + 2, far_to[h][0])
        arrived(dxf.at[k], k, DOT_X, to_xb)
        move(dxf.at[k], dxo.at[k], k, DOT_X + 2, to_xf)

    def rs2(k):
        for h in range(2):
            arrived(rb.at[k, h], k, RS_R1 + 3 * h + 1, far_to[h][0])
            arrived(rc.at[k, h], k, RS_R1 + 3 * h + 2, far_to[h][1])
            rsum[k, h] = add(chip_line(k, h, far_at[h][0])[...], rb[k, h], rc[k, h]).astype(BF16)
            move(rsum.at[k, h, near_at[h][3]], qa.at[k, h], k, RS_R2 + 3 * h, near_to[h][0])
            move(rsum.at[k, h, near_at[h][1]], qb.at[k, h], k, RS_R2 + 3 * h + 1, near_to[h][1])
        arrived(dxb.at[k], k, DOT_X + 1, to_xf)
        arrived(dxo.at[k], k, DOT_X + 2, to_xb)
        dr[k] = ds[k] + dxf[k] + dxb[k] + dxo[k]
        move(dr.at[k], dzf.at[k], k, DOT_Z, to_zf)
        move(dr.at[k], dzb.at[k], k, DOT_Z + 1, to_zb)

    def rs3(k):
        for h in range(2):
            arrived(qa.at[k, h], k, RS_R2 + 3 * h, near_to[h][1])
            qst[k, h] = add(qa[k, h], rsum[k, h, near_at[h][2]]).astype(BF16)
            move(qst.at[k, h], qc.at[k, h], k, RS_R2 + 3 * h + 2, near_to[h][0])
        arrived(dzf.at[k], k, DOT_Z, to_zb)
        move(dzf.at[k], dzo.at[k], k, DOT_Z + 2, to_zf)

    def rs4(k):
        arrived(dzb.at[k], k, DOT_Z + 1, to_zf)
        arrived(dzo.at[k], k, DOT_Z + 2, to_zb)
        dots = (dr[k] + dzf[k] + dzb[k] + dzo[k])[0:1]
        inverse = inv_s[k][0:1]
        pull = dots * inverse * inverse / D
        for h in range(2):
            arrived(qb.at[k, h], k, RS_R2 + 3 * h + 1, near_to[h][0])
            arrived(qc.at[k, h], k, RS_R2 + 3 * h + 2, near_to[h][1])
            norm_grad = add(rsum[k, h, near_at[h][0]], qb[k, h], qc[k, h])
            span = slice(h * HALF, (h + 1) * HALF)
            cols = slice(k * tok, (k + 1) * tok)
            full = og_own_ref[span, cols].astype(F32) + gain_own_ref[span, 0:1].astype(F32) * inverse * norm_grad
            full = full - res_ref[span, cols].astype(F32) * pull
            out_ref[span, cols] = full.astype(BF16)

    def wait_local(*which):
        for n in which:
            local[n].wait()

    for k in range(CHUNKS):
        ag1(k)
    hidden(0)
    ag2(0)
    hidden(1)
    ag3(0)
    ag2(1)
    hidden(2)
    ag3(1)
    ag2(2)
    hidden(3)
    ag4(0)
    hidden(4)
    ag3(2)
    hidden(5)
    ag5(0)
    hidden(6)
    ag4(1)
    hidden(7)
    wait_local(4, 0, 1)
    ag6(0)
    gates(0)
    ag5(1)
    ag4(2)
    wait_local(2, 3)
    last(0)
    ag6(1)
    gates(1)
    rs0(0)
    rs0b(0)
    ag5(2)
    last(1)
    rs1(0)
    ag6(2)
    gates(2)
    rs2(0)
    rs0(1)
    rs0b(1)
    last(2)
    rs3(0)
    rs1(1)
    rs4(0)
    rs0(2)
    rs0b(2)
    rs2(1)
    rs3(1)
    rs1(2)
    rs4(1)
    rs2(2)
    rs3(2)
    rs4(2)
    for copy in sent:
        copy.wait_send()


def core(residual, out_grad_t, gain_own, og_ext, w_down, w_gate, w_up):
    width = residual.shape[1]
    tok = width // CHUNKS
    hid = w_gate.shape[1]
    vm = pl.BlockSpec(memory_space=pltpu.VMEM)
    hbm = pl.BlockSpec(memory_space=pl.ANY)

    def bf(*shape):
        return pltpu.VMEM(shape, BF16)

    def fl(*shape):
        return pltpu.VMEM(shape, F32)

    rows = SIDE * 2 * 2 * HALF
    return pl.pallas_call(
        core_kernel,
        out_shape=jax.ShapeDtypeStruct(residual.shape, BF16),
        in_specs=[vm] * 3 + [hbm] * 6,
        out_specs=vm,
        scratch_shapes=[
            bf(CHUNKS, SIDE, SIDE, 2, 2, HALF, tok),
            bf(D, hid), bf(D, hid), bf(hid, D), bf(hid, D),
            bf(D, 128),
            bf(2, KB, width), bf(2, hid, KB),
            fl(hid, width),
            bf(rows, tok), fl(hid, tok), fl(hid, tok), bf(2 * hid, tok), fl(CHUNKS, 8, tok),
            bf(CHUNKS, SIDE, SIDE, 2, 2, HALF, tok), bf(CHUNKS, SIDE, SIDE, 2, HALF, tok),
        ]
        + [bf(CHUNKS, 2, SIDE, HALF, tok)] * 5
        + [bf(CHUNKS, 2, HALF, tok)] * 4
        + [fl(CHUNKS, 8, tok)] * 10
        + [
            pltpu.SemaphoreType.DMA((CHUNKS, SLOTS)),
            pltpu.SemaphoreType.DMA((CHUNKS, SLOTS)),
            pltpu.SemaphoreType.DMA((5,)),
            pltpu.SemaphoreType.DMA((2, 2)),
        ],
        compiler_params=pltpu.CompilerParams(
            collective_id=0, has_side_effects=True, vmem_limit_bytes=60 * 1024 * 1024
        ),
        cost_estimate=pl.CostEstimate(flops=10 * D * hid * width, bytes_accessed=40_000_000, transcendentals=0),
        name="core",
    )(residual, out_grad_t, gain_own, og_ext, w_down, w_gate, w_up, w_gate.T, w_up.T)


def per_device(tokens_in, out_grad, tenant, slot_of, steer_table, norm_gain, w_gate, w_up, w_down):
    holders = lax.axis_size(("dp", "tensor"))
    groups = lax.axis_size("dp")
    width_parts = lax.axis_size("tensor")
    rows_own = steer_table.shape[0]
    feat_local = tokens_in.shape[1]
    token_count = tenant.shape[0]
    capacity = 4 * token_count // holders
    group = lax.axis_index("dp")
    me = lax.axis_index(("dp", "tensor"))

    tenant_all = lax.all_gather(tenant, "dp", axis=0, tiled=True)
    out_grad_t = out_grad.T
    gain_own = jnp.broadcast_to(norm_gain[:, None], (feat_local, 128))
    og_ext = lax.all_gather(jnp.concatenate([out_grad_t, gain_own], axis=1), "tensor", axis=0, tiled=True)

    owners_all, rows_all = look_up_slots(slot_of, tenant_all)
    earlier = (
        jnp.arange(token_count, dtype=jnp.int32)[:, None] < jnp.arange(token_count, dtype=jnp.int32)[None, :]
    ).astype(BF16)
    mine = (owners_all == me).reshape(groups, token_count)
    rank_mine = dot(mine.astype(BF16), earlier, 1, 0).astype(jnp.int32)
    slot_of_token = jnp.where(mine, rank_mine, -1)
    slots = (slot_of_token[:, None, :] == jnp.arange(capacity, dtype=jnp.int32)[None, :, None]).astype(BF16)
    row_hot = one_hot(rows_all.reshape(groups, token_count), rows_own).astype(BF16)
    wanted = lax.dot_general(slots, row_hot, (((2,), (1,)), ((0,), (0,))), preferred_element_type=F32)
    wanted = wanted.astype(BF16).reshape(groups * capacity, rows_own)
    picked = dot(wanted, steer_table, 1, 0).astype(BF16)
    outgoing = picked.reshape(groups, capacity, width_parts, feat_local).transpose(0, 2, 1, 3)
    outgoing = outgoing.reshape(holders, capacity, feat_local)
    returned = lax.all_to_all(outgoing, ("dp", "tensor"), split_axis=0, concat_axis=0, tiled=True)
    returned = returned.reshape(holders * capacity, feat_local)

    owners = lax.dynamic_slice_in_dim(owners_all, group * token_count, token_count)
    matches = one_hot(owners, holders).astype(BF16)
    before = dot(earlier, matches, 0, 0)
    ranking = jnp.sum(jnp.where(matches > 0, before, 0.0), axis=1).astype(jnp.int32)
    place = one_hot(owners * capacity + ranking, holders * capacity).astype(BF16)
    steering = dot(returned, place, 0, 1)

    residual = (tokens_in.T.astype(F32) + steering).astype(BF16)
    full_grad = core(residual, out_grad_t, gain_own, og_ext, w_down, w_gate, w_up)

    sending = dot(place, full_grad, 0, 1).astype(BF16).reshape(holders, capacity, feat_local)
    received = lax.all_to_all(sending, ("dp", "tensor"), split_axis=0, concat_axis=0, tiled=True)
    received = received.reshape(groups, width_parts, capacity, feat_local).transpose(0, 2, 1, 3)
    received = received.reshape(groups * capacity, width_parts * feat_local)
    table_grad = dot(wanted, received, 0, 0)
    return (full_grad.T, table_grad)


def solution(mesh):
    placed = (
        P("dp", "tensor"),
        P("dp", "tensor"),
        P("dp"),
        P(),
        P(("dp", "tensor"), None),
        P("tensor"),
        P(None, "tensor"),
        P(None, "tensor"),
        P("tensor", None),
    )
    return jax.shard_map(
        per_device,
        mesh=mesh,
        in_specs=placed,
        out_specs=(P("dp", "tensor"), P(("dp", "tensor"), None)),
        check_vma=False,
    )
```

```python
import functools

import jax
import jax.numpy as jnp
from jax import lax
from jax.experimental import pallas as pl
from jax.experimental.pallas import tpu as pltpu
from jax.sharding import PartitionSpec as P

D = 5120
F32 = jnp.float32
BF16 = jnp.bfloat16


CHUNKS = 3
SIDE = 4
HALF = 80
KB = 640
AG_P1 = 0
AG_P2 = 6
AG_SIB = 12
RS_SIB = 20
RS_R1 = 24
RS_R2 = 30
DOT_SIB = 36
DOT_X = 37
DOT_Z = 40
SLOTS = 43


def core_kernel(
    res_ref, og_own_ref, gain_own_ref, og_hbm, wd_hbm, wg_hbm, wu_hbm, wgt_hbm, wut_hbm,
    out_ref,
    x_all, wg, wu, wgt, wut, gain, og_buf, wd_buf, hid, y_buf, g_acc, u_acc, both, inv_s,
    part, sib_in, ra, rb, rc, rst, rsum, qa, qb, qc, qst,
    dp_, ds, dq, dxf, dxb, dxo, dr, dzf, dzb, dzo,
    ssem, rsem, lsem, hsem,
):
    ten = lax.axis_index("tensor")
    x = ten // 8
    z = lax.rem(ten // 2, 4)
    c = lax.rem(ten, 2)
    step = 1 - 2 * c
    xf, xb, xo = lax.rem(x + step + 4, 4), lax.rem(x - step + 4, 4), lax.rem(x + 2, 4)
    zf, zb, zo = lax.rem(z + step + 4, 4), lax.rem(z - step + 4, 4), lax.rem(z + 2, 4)

    def dev(xx, zz, cc):
        return {"tensor": (xx * 4 + zz) * 2 + cc}

    to_xf, to_xb = dev(xf, z, c), dev(xb, z, c)
    to_zf, to_zb = dev(x, zf, c), dev(x, zb, c)
    to_sib = dev(x, z, 1 - c)
    width = res_ref.shape[1]
    tok = width // CHUNKS
    rows = SIDE * 2 * 2 * HALF

    local = [
        pltpu.make_async_copy(wgt_hbm, wgt, lsem.at[0]),
        pltpu.make_async_copy(wut_hbm, wut, lsem.at[1]),
        pltpu.make_async_copy(wg_hbm, wg, lsem.at[2]),
        pltpu.make_async_copy(wu_hbm, wu, lsem.at[3]),
        pltpu.make_async_copy(og_hbm.at[:, pl.ds(width, 128)], gain, lsem.at[4]),
    ]

    def hidden_copies(j):
        return (
            pltpu.make_async_copy(og_hbm.at[pl.ds(j * KB, KB), pl.ds(0, width)], og_buf.at[j % 2], hsem.at[0, j % 2]),
            pltpu.make_async_copy(wd_hbm.at[:, pl.ds(j * KB, KB)], wd_buf.at[j % 2], hsem.at[1, j % 2]),
        )

    for copy in hidden_copies(0) + hidden_copies(1):
        copy.start()
    for copy in local:
        copy.start()

    for k in range(CHUNKS):
        for h in range(2):
            x_all[k, x, z, c, h] = res_ref[h * HALF:(h + 1) * HALF, k * tok:(k + 1) * tok]

    barrier = pltpu.get_barrier_semaphore()
    for where in (to_xf, to_xb, to_zf, to_zb, to_sib):
        pl.semaphore_signal(barrier, inc=1, device_id=where, device_id_type=pl.DeviceIdType.MESH)
    pl.semaphore_wait(barrier, 5)

    sent = []

    def move(src, dst, k, slot, where):
        copy = pltpu.make_async_remote_copy(
            src_ref=src, dst_ref=dst, send_sem=ssem.at[k, slot], recv_sem=rsem.at[k, slot],
            device_id=where, device_id_type=pl.DeviceIdType.MESH,
        )
        copy.start()
        sent.append(copy)

    def arrived(dst, k, slot, where):
        pltpu.make_async_remote_copy(
            src_ref=dst, dst_ref=dst, send_sem=ssem.at[k, slot], recv_sem=rsem.at[k, slot],
            device_id=where, device_id_type=pl.DeviceIdType.MESH,
        ).wait_recv()

    def one(k, xx, zz, h):
        return x_all.at[k, xx, zz, c, h]

    def line(k, h, at, cc):
        return x_all.at[k, at, :, cc, 0] if h == 0 else x_all.at[k, :, at, cc, 1]

    near_to = ((to_zf, to_zb), (to_xf, to_xb))
    far_to = ((to_xf, to_xb), (to_zf, to_zb))
    far_at = ((x, xb, xf, xo), (z, zb, zf, zo))

    def near(k, h, at):
        return one(k, x, at, 0) if h == 0 else one(k, at, z, 1)

    near_at = ((z, zb, zf, zo), (x, xb, xf, xo))

    def ag1(k):
        for h in range(2):
            own = one(k, x, z, h)
            move(own, own, k, AG_P1 + 3 * h, near_to[h][0])
            move(own, own, k, AG_P1 + 3 * h + 1, near_to[h][1])

    def ag2(k):
        for h in range(2):
            behind = near(k, h, near_at[h][1])
            arrived(behind, k, AG_P1 + 3 * h, near_to[h][1])
            move(behind, behind, k, AG_P1 + 3 * h + 2, near_to[h][0])

    def ag3(k):
        for h in range(2):
            arrived(near(k, h, near_at[h][2]), k, AG_P1 + 3 * h + 1, near_to[h][0])
            arrived(near(k, h, near_at[h][3]), k, AG_P1 + 3 * h + 2, near_to[h][1])
            own = line(k, h, far_at[h][0], c)
            move(own, own, k, AG_P2 + 3 * h, far_to[h][0])
            move(own, own, k, AG_P2 + 3 * h + 1, far_to[h][1])
            move(own, own, k, AG_SIB + 4 * h, to_sib)

    def ag4(k):
        for h in range(2):
            behind = line(k, h, far_at[h][1], c)
            arrived(behind, k, AG_P2 + 3 * h, far_to[h][1])
            move(behind, behind, k, AG_P2 + 3 * h + 2, far_to[h][0])
            move(behind, behind, k, AG_SIB + 4 * h + 1, to_sib)
        for h in range(2):
            ahead = line(k, h, far_at[h][2], c)
            arrived(ahead, k, AG_P2 + 3 * h + 1, far_to[h][0])
            move(ahead, ahead, k, AG_SIB + 4 * h + 2, to_sib)

    def ag5(k):
        for h in range(2):
            opposite = line(k, h, far_at[h][3], c)
            arrived(opposite, k, AG_P2 + 3 * h + 2, far_to[h][1])
            move(opposite, opposite, k, AG_SIB + 4 * h + 3, to_sib)

    def ag6(k):
        for h in range(2):
            at = far_at[h]
            for n, i in enumerate((0, 2, 1, 3)):
                arrived(line(k, h, at[i], 1 - c), k, AG_SIB + 4 * h + n, to_sib)

    def hidden(j):
        for copy in hidden_copies(j):
            copy.wait()
        part_sum = jnp.dot(wd_buf[j % 2], og_buf[j % 2], preferred_element_type=F32)
        if j == 0:
            hid[...] = part_sum
        else:
            hid[...] += part_sum
        if j + 2 < D // KB:
            for copy in hidden_copies(j + 2):
                copy.start()

    def gates(k):
        g_acc[...] = jnp.zeros_like(g_acc)
        u_acc[...] = jnp.zeros_like(u_acc)

        def body(i, squares):
            at = pl.multiple_of(i * rows, rows)
            wide = x_all[k, i].reshape(rows, tok).astype(F32)
            scale = gain[pl.ds(at, rows), :].astype(F32)
            scale = jnp.concatenate([scale] * (tok // 128), axis=1)
            y_buf[...] = (wide * scale).astype(BF16)
            g_acc[...] += jnp.dot(wgt[:, pl.ds(at, rows)], y_buf[...], preferred_element_type=F32)
            u_acc[...] += jnp.dot(wut[:, pl.ds(at, rows)], y_buf[...], preferred_element_type=F32)
            return squares + jnp.sum(wide * wide, axis=0, keepdims=True)

        squares = lax.fori_loop(0, SIDE, body, jnp.zeros((1, tok), F32))
        inverse = lax.rsqrt(squares / D + 1e-06)
        inv_s[k] = jnp.broadcast_to(inverse, (8, tok))
        gate_out = g_acc[...] * inverse
        up_out = u_acc[...] * inverse
        hidden_grad = hid[:, k * tok:(k + 1) * tok]
        sigma = jax.nn.sigmoid(gate_out)
        gate_grad = (hidden_grad * up_out * (sigma * (1.0 + gate_out * (1.0 - sigma)))).astype(BF16)
        up_grad = (hidden_grad * (gate_out * sigma)).astype(BF16)
        half = gate_grad.shape[0]
        both[0:half] = gate_grad
        both[half:2 * half] = up_grad
        dots = jnp.sum(gate_grad.astype(F32) * gate_out + up_grad.astype(F32) * up_out, axis=0, keepdims=True)
        dp_[k] = jnp.broadcast_to(dots, (8, tok))
        move(dp_.at[k], dq.at[k], k, DOT_SIB, to_sib)

    def last(k):
        half = both.shape[0] // 2

        for i in range(SIDE):
            at = i * rows
            term = jnp.dot(wg[at:at + rows, :], both[0:half], preferred_element_type=F32)
            term = term + jnp.dot(wu[at:at + rows, :], both[half:2 * half], preferred_element_type=F32)
            part[k, i] = term.astype(BF16).reshape(SIDE, 2, 2, HALF, tok)
            move(part.at[k, i, :, 1 - c], sib_in.at[k, i], k, RS_SIB + i, to_sib)

    def add(*refs_):
        total = refs_[0].astype(F32)
        for other in refs_[1:]:
            total = total + other.astype(F32)
        return total

    def chip_line(k, h, at):
        return part.at[k, at, :, c, 0] if h == 0 else part.at[k, :, at, c, 1]

    def rs0(k):
        for i in range(SIDE):
            arrived(sib_in.at[k, i], k, RS_SIB + i, to_sib)
            part[k, i, :, c] = add(part[k, i, :, c], sib_in[k, i]).astype(BF16)
        for h in range(2):
            move(chip_line(k, h, far_at[h][3]), ra.at[k, h], k, RS_R1 + 3 * h, far_to[h][0])
        for h in range(2):
            move(chip_line(k, h, far_at[h][1]), rb.at[k, h], k, RS_R1 + 3 * h + 1, far_to[h][1])
        arrived(dq.at[k], k, DOT_SIB, to_sib)
        ds[k] = dp_[k] + dq[k]

    def rs0b(k):
        move(ds.at[k], dxf.at[k], k, DOT_X, to_xf)
        move(ds.at[k], dxb.at[k], k, DOT_X + 1, to_xb)

    def rs1(k):
        for h in range(2):
            arrived(ra.at[k, h], k, RS_R1 + 3 * h, far_to[h][1])
            rst[k, h] = add(ra[k, h], chip_line(k, h, far_at[h][2])[...]).astype(BF16)
            move(rst.at[k, h], rc.at[k, h], k, RS_R1 + 3 * h + 2, far_to[h][0])
        arrived(dxf.at[k], k, DOT_X, to_xb)
        move(dxf.at[k], dxo.at[k], k, DOT_X + 2, to_xf)

    def rs2(k):
        for h in range(2):
            arrived(rb.at[k, h], k, RS_R1 + 3 * h + 1, far_to[h][0])
            arrived(rc.at[k, h], k, RS_R1 + 3 * h + 2, far_to[h][1])
            rsum[k, h] = add(chip_line(k, h, far_at[h][0])[...], rb[k, h], rc[k, h]).astype(BF16)
            move(rsum.at[k, h, near_at[h][3]], qa.at[k, h], k, RS_R2 + 3 * h, near_to[h][0])
            move(rsum.at[k, h, near_at[h][1]], qb.at[k, h], k, RS_R2 + 3 * h + 1, near_to[h][1])
        arrived(dxb.at[k], k, DOT_X + 1, to_xf)
        arrived(dxo.at[k], k, DOT_X + 2, to_xb)
        dr[k] = ds[k] + dxf[k] + dxb[k] + dxo[k]
        move(dr.at[k], dzf.at[k], k, DOT_Z, to_zf)
        move(dr.at[k], dzb.at[k], k, DOT_Z + 1, to_zb)

    def rs3(k):
        for h in range(2):
            arrived(qa.at[k, h], k, RS_R2 + 3 * h, near_to[h][1])
            qst[k, h] = add(qa[k, h], rsum[k, h, near_at[h][2]]).astype(BF16)
            move(qst.at[k, h], qc.at[k, h], k, RS_R2 + 3 * h + 2, near_to[h][0])
        arrived(dzf.at[k], k, DOT_Z, to_zb)
        move(dzf.at[k], dzo.at[k], k, DOT_Z + 2, to_zf)

    def rs4(k):
        arrived(dzb.at[k], k, DOT_Z + 1, to_zf)
        arrived(dzo.at[k], k, DOT_Z + 2, to_zb)
        dots = (dr[k] + dzf[k] + dzb[k] + dzo[k])[0:1]
        inverse = inv_s[k][0:1]
        pull = dots * inverse * inverse / D
        for h in range(2):
            arrived(qb.at[k, h], k, RS_R2 + 3 * h + 1, near_to[h][0])
            arrived(qc.at[k, h], k, RS_R2 + 3 * h + 2, near_to[h][1])
            norm_grad = add(rsum[k, h, near_at[h][0]], qb[k, h], qc[k, h])
            span = slice(h * HALF, (h + 1) * HALF)
            cols = slice(k * tok, (k + 1) * tok)
            full = og_own_ref[span, cols].astype(F32) + gain_own_ref[span, 0:1].astype(F32) * inverse * norm_grad
            full = full - res_ref[span, cols].astype(F32) * pull
            out_ref[span, cols] = full.astype(BF16)

    def wait_local(*which):
        for n in which:
            local[n].wait()

    for k in range(CHUNKS):
        ag1(k)
    hidden(0)
    ag2(0)
    hidden(1)
    ag3(0)
    ag2(1)
    hidden(2)
    ag3(1)
    ag2(2)
    hidden(3)
    ag4(0)
    hidden(4)
    ag3(2)
    hidden(5)
    ag5(0)
    hidden(6)
    ag4(1)
    hidden(7)
    wait_local(4, 0, 1)
    ag6(0)
    gates(0)
    ag5(1)
    ag4(2)
    wait_local(2, 3)
    last(0)
    ag6(1)
    gates(1)
    rs0(0)
    rs0b(0)
    ag5(2)
    last(1)
    rs1(0)
    ag6(2)
    gates(2)
    rs2(0)
    rs0(1)
    rs0b(1)
    last(2)
    rs3(0)
    rs1(1)
    rs4(0)
    rs0(2)
    rs0b(2)
    rs2(1)
    rs3(1)
    rs1(2)
    rs4(1)
    rs2(2)
    rs3(2)
    rs4(2)
    for copy in sent:
        copy.wait_send()


def core(residual, out_grad_t, gain_own, og_ext, w_down, w_gate, w_up):
    width = residual.shape[1]
    tok = width // CHUNKS
    hid = w_gate.shape[1]
    vm = pl.BlockSpec(memory_space=pltpu.VMEM)
    hbm = pl.BlockSpec(memory_space=pl.ANY)

    def bf(*shape):
        return pltpu.VMEM(shape, BF16)

    def fl(*shape):
        return pltpu.VMEM(shape, F32)

    rows = SIDE * 2 * 2 * HALF
    return pl.pallas_call(
        core_kernel,
        out_shape=jax.ShapeDtypeStruct(residual.shape, BF16),
        in_specs=[vm] * 3 + [hbm] * 6,
        out_specs=vm,
        scratch_shapes=[
            bf(CHUNKS, SIDE, SIDE, 2, 2, HALF, tok),
            bf(D, hid), bf(D, hid), bf(hid, D), bf(hid, D),
            bf(D, 128),
            bf(2, KB, width), bf(2, hid, KB),
            fl(hid, width),
            bf(rows, tok), fl(hid, tok), fl(hid, tok), bf(2 * hid, tok), fl(CHUNKS, 8, tok),
            bf(CHUNKS, SIDE, SIDE, 2, 2, HALF, tok), bf(CHUNKS, SIDE, SIDE, 2, HALF, tok),
        ]
        + [bf(CHUNKS, 2, SIDE, HALF, tok)] * 5
        + [bf(CHUNKS, 2, HALF, tok)] * 4
        + [fl(CHUNKS, 8, tok)] * 10
        + [
            pltpu.SemaphoreType.DMA((CHUNKS, SLOTS)),
            pltpu.SemaphoreType.DMA((CHUNKS, SLOTS)),
            pltpu.SemaphoreType.DMA((5,)),
            pltpu.SemaphoreType.DMA((2, 2)),
        ],
        compiler_params=pltpu.CompilerParams(
            collective_id=0, has_side_effects=True, vmem_limit_bytes=60 * 1024 * 1024
        ),
        cost_estimate=pl.CostEstimate(flops=10 * D * hid * width, bytes_accessed=40_000_000, transcendentals=0),
        name="core",
    )(residual, out_grad_t, gain_own, og_ext, w_down, w_gate, w_up, w_gate.T, w_up.T)


MESH = pl.DeviceIdType.MESH
SLOT = 32
SPANS = ((0, 512), (512, 384))


def nt(a, b):
    return lax.dot_general(a, b, (((1,), (1,)), ((), ())), preferred_element_type=F32)


def fetch_kernel(
    tok_ref, og_ref, ten_ref, halves_ref, table_ref,
    res_ref, og_out, wanted_ref, place_ref,
    tbuf, earlier, rows_s, rows_r, turned, landed, acc,
    tsend, trecv, ysend, yrecv, psend, precv, gsend, grecv, lsem,
):
    d = lax.axis_index("dp")
    t = lax.axis_index("tensor")
    me = d * 32 + t
    x = t // 8
    z = lax.rem(t // 2, 4)
    c = lax.rem(t, 2)
    step = 1 - 2 * c
    xf, xb, xo = lax.rem(x + step + 4, 4), lax.rem(x - step + 4, 4), lax.rem(x + 2, 4)
    zf, zb, zo = lax.rem(z + step + 4, 4), lax.rem(z - step + 4, 4), lax.rem(z + 2, 4)

    def dev(xx, zz, cc):
        return {"dp": d, "tensor": (xx * 4 + zz) * 2 + cc}

    to_xf, to_xb = dev(xf, z, c), dev(xb, z, c)
    to_zf, to_zb = dev(x, zf, c), dev(x, zb, c)
    to_sib = dev(x, z, 1 - c)
    width = tok_ref.shape[1]
    feat = tok_ref.shape[0]
    parts = D // feat

    own_copies = [
        pltpu.make_async_copy(og_ref.at[pl.ds(h * HALF, HALF)], og_out.at[x, z, c, h], lsem.at[h]) for h in range(2)
    ]
    for copy in own_copies:
        copy.start()
    barrier = pltpu.get_barrier_semaphore()

    def greet(o, carry):
        pl.semaphore_signal(
            barrier, inc=1, device_id={"dp": d, "tensor": lax.rem(t + o, parts)}, device_id_type=MESH
        )
        return carry

    lax.fori_loop(1, parts, greet, 0)
    for o in (1, 2, 3):
        pl.semaphore_signal(barrier, inc=1, device_id={"dp": lax.rem(d + o, 4), "tensor": t}, device_id_type=MESH)
    pl.semaphore_wait(barrier, parts - 1 + 3)

    sent = []

    def send(src, dst, ssem, rsem, where):
        copy = pltpu.make_async_remote_copy(
            src_ref=src, dst_ref=dst, send_sem=ssem, recv_sem=rsem, device_id=where, device_id_type=MESH
        )
        copy.start()
        sent.append(copy)

    def got(dst, ssem, rsem, where):
        pltpu.make_async_remote_copy(
            src_ref=dst, dst_ref=dst, send_sem=ssem, recv_sem=rsem, device_id=where, device_id_type=MESH
        ).wait_recv()

    for o in (1, 3, 2):
        there = lax.rem(d + o, 4)
        send(ten_ref, tbuf.at[d], tsend.at[there], trecv.at[d], {"dp": there, "tensor": t})

    near_to = ((to_zf, to_zb), (to_xf, to_xb))
    far_to = ((to_xf, to_xb), (to_zf, to_zb))
    near_at = ((z, zb, zf, zo), (x, xb, xf, xo))
    far_at = ((x, xb, xf, xo), (z, zb, zf, zo))

    def lanes(k):
        return pl.ds(SPANS[k][0], SPANS[k][1])

    def near(k, h, at):
        return og_out.at[x, at, c, 0, :, lanes(k)] if h == 0 else og_out.at[at, z, c, 1, :, lanes(k)]

    def line(k, h, at, cc):
        return og_out.at[at, :, cc, 0, :, lanes(k)] if h == 0 else og_out.at[:, at, cc, 1, :, lanes(k)]

    def move(src, dst, k, slot, where):
        send(src, dst, gsend.at[k, slot], grecv.at[k, slot], where)

    def arrived(dst, k, slot, where):
        got(dst, gsend.at[k, slot], grecv.at[k, slot], where)

    def ag1(k):
        for h in range(2):
            own = near(k, h, near_at[h][0])
            src = og_ref.at[pl.ds(h * HALF, HALF), lanes(k)]
            move(src, own, k, AG_P1 + 3 * h, near_to[h][0])
            move(src, own, k, AG_P1 + 3 * h + 1, near_to[h][1])

    def ag2(k):
        for h in range(2):
            behind = near(k, h, near_at[h][1])
            arrived(behind, k, AG_P1 + 3 * h, near_to[h][1])
            move(behind, behind, k, AG_P1 + 3 * h + 2, near_to[h][0])

    def ag3(k):
        for h in range(2):
            arrived(near(k, h, near_at[h][2]), k, AG_P1 + 3 * h + 1, near_to[h][0])
            arrived(near(k, h, near_at[h][3]), k, AG_P1 + 3 * h + 2, near_to[h][1])
            own = line(k, h, far_at[h][0], c)
            move(own, own, k, AG_P2 + 3 * h, far_to[h][0])
            move(own, own, k, AG_P2 + 3 * h + 1, far_to[h][1])
            move(own, own, k, AG_SIB + 4 * h, to_sib)

    def ag4(k):
        for h in range(2):
            behind = line(k, h, far_at[h][1], c)
            arrived(behind, k, AG_P2 + 3 * h, far_to[h][1])
            move(behind, behind, k, AG_P2 + 3 * h + 2, far_to[h][0])
            move(behind, behind, k, AG_SIB + 4 * h + 1, to_sib)
        for h in range(2):
            ahead = line(k, h, far_at[h][2], c)
            arrived(ahead, k, AG_P2 + 3 * h + 1, far_to[h][0])
            move(ahead, ahead, k, AG_SIB + 4 * h + 2, to_sib)

    def ag5(k):
        for h in range(2):
            opposite = line(k, h, far_at[h][3], c)
            arrived(opposite, k, AG_P2 + 3 * h + 2, far_to[h][1])
            move(opposite, opposite, k, AG_SIB + 4 * h + 3, to_sib)

    def ag6(k):
        for h in range(2):
            for n, i in enumerate((0, 2, 1, 3)):
                arrived(line(k, h, far_at[h][i], 1 - c), k, AG_SIB + 4 * h + n, to_sib)

    ag1(0)
    ag1(1)

    lines = halves_ref.shape[1]
    earlier[...] = (
        lax.broadcasted_iota(jnp.int32, (width, width), 0) < lax.broadcasted_iota(jnp.int32, (width, width), 1)
    ).astype(F32).astype(BF16)

    def hot(index, size):
        return (lax.broadcasted_iota(jnp.int32, (size, width), 0) == index).astype(F32)

    def look_up(tenant):
        picked = jnp.dot(halves_ref[...], hot(tenant // 128, lines).astype(BF16), preferred_element_type=F32)
        lane = hot(lax.rem(tenant, 128), 128)
        owner = jnp.sum(lane * picked[:128], axis=0, keepdims=True).astype(jnp.int32)
        row = jnp.sum(lane * picked[128:], axis=0, keepdims=True).astype(jnp.int32)
        return owner, row

    def ranks(matches):
        before = jnp.dot(matches.astype(BF16), earlier[...], preferred_element_type=F32)
        return jnp.sum(matches * before, axis=0, keepdims=True).astype(jnp.int32)

    owner, row = look_up(ten_ref[0:1])
    rank = ranks(hot(owner, 128))
    place = lax.rem(owner, 32) * 128 + owner // 32 * SLOT + rank
    place_ref[...] = jnp.broadcast_to(place, place_ref.shape)
    ag2(0)
    ag2(1)

    tbuf[d] = ten_ref[...]
    for o in (1, 3, 2):
        there = lax.rem(d + o, 4)
        got(tbuf.at[there], tsend.at[there], trecv.at[there], {"dp": there, "tensor": t})
    for g in range(4):
        owner, row = look_up(tbuf[g, 0:1])
        mine = (owner == me).astype(F32)
        mine8 = jnp.broadcast_to(mine, (8, width))
        before = jnp.dot(mine8.astype(BF16), earlier[...], preferred_element_type=F32)[0:1]
        slot = jnp.where(mine > 0, before.astype(jnp.int32), -1)
        wanted = nt(hot(slot, SLOT).astype(BF16), hot(row, table_ref.shape[0]).astype(BF16)).astype(BF16)
        wanted_ref[g * SLOT:(g + 1) * SLOT] = wanted
        rows_s[g] = jnp.dot(wanted, table_ref[...], preferred_element_type=F32).astype(BF16)
    for o in (1, 3, 2):
        there = lax.rem(d + o, 4)
        send(rows_s.at[there], rows_r.at[d], ysend.at[there], yrecv.at[d], {"dp": there, "tensor": t})
    rows_r[d] = rows_s[d]
    for copy in own_copies:
        copy.wait()
    ag3(0)
    ag3(1)
    ag4(0)
    for o in (3, 1, 2):
        there = lax.rem(d + o, 4)
        got(rows_r.at[there], ysend.at[there], yrecv.at[there], {"dp": there, "tensor": t})
    wide = 640

    def turn(i, carry):
        at = pl.multiple_of(i * wide, wide)
        block = rows_r[:, :, pl.ds(at, wide)].reshape(4 * SLOT, wide)
        turned[pl.ds(at, wide), :] = block.T
        return carry

    lax.fori_loop(0, D // wide, turn, 0)

    def scatter(o, carry):
        there = lax.rem(t + o, parts)
        pltpu.make_async_remote_copy(
            src_ref=turned.at[pl.ds(pl.multiple_of(there * feat, 16), feat)], dst_ref=landed.at[t],
            send_sem=psend.at[there], recv_sem=precv.at[t],
            device_id={"dp": d, "tensor": there}, device_id_type=MESH,
        ).start()
        return carry

    lax.fori_loop(1, parts, scatter, 0)
    landed[t] = turned[pl.ds(pl.multiple_of(t * feat, 16), feat), :]
    acc[...] = tok_ref[...].astype(F32)
    ag4(1)
    ag5(0)

    def add_from(src):
        sel = (lax.broadcasted_iota(jnp.int32, (128, width), 0) + src * 128 == place).astype(F32).astype(BF16)
        acc[...] += jnp.dot(landed[src], sel, preferred_element_type=F32)

    add_from(t)

    def gather(o, carry):
        src = lax.rem(t + parts - o, parts)
        pltpu.make_async_remote_copy(
            src_ref=landed.at[src], dst_ref=landed.at[src],
            send_sem=psend.at[src], recv_sem=precv.at[src],
            device_id={"dp": d, "tensor": src}, device_id_type=MESH,
        ).wait_recv()
        add_from(src)
        return carry

    lax.fori_loop(1, parts, gather, 0)
    res_ref[...] = acc[...].astype(BF16)
    ag5(1)
    ag6(0)
    ag6(1)

    def drain(o, carry):
        there = lax.rem(t + o, parts)
        pltpu.make_async_remote_copy(
            src_ref=turned.at[pl.ds(pl.multiple_of(there * feat, 16), feat)], dst_ref=landed.at[t],
            send_sem=psend.at[there], recv_sem=precv.at[t],
            device_id={"dp": d, "tensor": there}, device_id_type=MESH,
        ).wait_send()
        return carry

    lax.fori_loop(1, parts, drain, 0)
    for copy in sent:
        copy.wait_send()


def fetch(tokens_t, og_ext, tenant8, halves, table):
    feat, width = tokens_t.shape
    parts = D // feat
    vm = pl.BlockSpec(memory_space=pltpu.VMEM)
    dma = pltpu.SemaphoreType.DMA
    return pl.pallas_call(
        fetch_kernel,
        out_shape=(
            jax.ShapeDtypeStruct((feat, width), BF16),
            jax.ShapeDtypeStruct((SIDE, SIDE, 2, 2, HALF, og_ext.shape[1]), BF16),
            jax.ShapeDtypeStruct((4 * SLOT, table.shape[0]), BF16),
            jax.ShapeDtypeStruct((8, width), jnp.int32),
        ),
        in_specs=[vm] * 5,
        out_specs=(vm, pl.BlockSpec(memory_space=pl.ANY), vm, vm),
        scratch_shapes=[
            pltpu.VMEM((4, 8, width), jnp.int32),
            pltpu.VMEM((width, width), BF16),
            pltpu.VMEM((4, SLOT, D), BF16),
            pltpu.VMEM((4, SLOT, D), BF16),
            pltpu.VMEM((D, 4 * SLOT), BF16),
            pltpu.VMEM((parts, feat, 4 * SLOT), BF16),
            pltpu.VMEM((feat, width), F32),
            dma((4,)), dma((4,)), dma((4,)), dma((4,)), dma((parts,)), dma((parts,)),
            dma((len(SPANS), RS_SIB)), dma((len(SPANS), RS_SIB)), dma((2,)),
        ],
        compiler_params=pltpu.CompilerParams(
            collective_id=1, has_side_effects=True, vmem_limit_bytes=48 * 1024 * 1024
        ),
        cost_estimate=pl.CostEstimate(flops=4_000_000_000, bytes_accessed=20_000_000, transcendentals=0),
        name="fetch",
    )(tokens_t, og_ext, tenant8, halves, table)


def give_kernel(full_ref, place_ref, rows_r, leaving, landed, rows_s, psend, precv, ysend, yrecv):
    d = lax.axis_index("dp")
    t = lax.axis_index("tensor")
    feat, width = full_ref.shape
    parts = D // feat
    barrier = pltpu.get_barrier_semaphore()

    def greet(o, carry):
        pl.semaphore_signal(
            barrier, inc=1, device_id={"dp": d, "tensor": lax.rem(t + o, parts)}, device_id_type=MESH
        )
        return carry

    lax.fori_loop(1, parts, greet, 0)
    for o in (1, 2, 3):
        pl.semaphore_signal(barrier, inc=1, device_id={"dp": lax.rem(d + o, 4), "tensor": t}, device_id_type=MESH)

    place = place_ref[0:1]

    def pack(there):
        sel = (lax.broadcasted_iota(jnp.int32, (4 * SLOT, width), 0) + there * 128 == place).astype(F32).astype(BF16)
        return nt(full_ref[...], sel).astype(BF16)

    landed[t] = pack(t)
    pl.semaphore_wait(barrier, parts - 1 + 3)

    def plane_copy(there, at):
        return pltpu.make_async_remote_copy(
            src_ref=leaving.at[there], dst_ref=landed.at[at], send_sem=psend.at[there], recv_sem=precv.at[at],
            device_id={"dp": d, "tensor": there}, device_id_type=MESH,
        )

    def scatter(o, carry):
        there = lax.rem(t + o, parts)
        leaving[there] = pack(there)
        plane_copy(there, t).start()
        return carry

    lax.fori_loop(1, parts, scatter, 0)

    group = 8

    def y_copy(q, there):
        return pltpu.make_async_remote_copy(
            src_ref=rows_s.at[q, there], dst_ref=rows_r.at[q, d], send_sem=ysend.at[q, there], recv_sem=yrecv.at[q, d],
            device_id={"dp": there, "tensor": t}, device_id_type=MESH,
        )

    def arrive(src):
        @pl.when(src != t)
        def _():
            pltpu.make_async_remote_copy(
                src_ref=landed.at[src], dst_ref=landed.at[src], send_sem=psend.at[src], recv_sem=precv.at[src],
                device_id={"dp": d, "tensor": src}, device_id_type=MESH,
            ).wait_recv()

    def quarter(n, carry):
        q = lax.rem(t // group + 4 - n, 4)

        def take(i, inner):
            arrive(q * group + i)
            return inner

        lax.fori_loop(0, group, take, 0)
        block = landed[pl.ds(q * group, group)].reshape(group * feat, 4 * SLOT)
        rows_s[q] = block.T.reshape(4, SLOT, group * feat)
        for o in (1, 3, 2):
            y_copy(q, lax.rem(d + o, 4)).start()
        rows_r[q, d] = rows_s[q, d]
        return carry

    lax.fori_loop(0, 4, quarter, 0)

    def finish(q, carry):
        for o in (1, 3, 2):
            there = lax.rem(d + o, 4)
            y_copy(q, there).wait_send()
            pltpu.make_async_remote_copy(
                src_ref=rows_r.at[q, there], dst_ref=rows_r.at[q, there],
                send_sem=ysend.at[q, there], recv_sem=yrecv.at[q, there],
                device_id={"dp": there, "tensor": t}, device_id_type=MESH,
            ).wait_recv()
        return carry

    lax.fori_loop(0, 4, finish, 0)

    def drain(o, carry):
        plane_copy(lax.rem(t + o, parts), t).wait_send()
        return carry

    lax.fori_loop(1, parts, drain, 0)


def give(full_grad, place):
    feat, width = full_grad.shape
    parts = D // feat
    vm = pl.BlockSpec(memory_space=pltpu.VMEM)
    dma = pltpu.SemaphoreType.DMA
    return pl.pallas_call(
        give_kernel,
        out_shape=jax.ShapeDtypeStruct((4, 4, SLOT, D // 4), BF16),
        in_specs=[vm] * 2,
        out_specs=vm,
        scratch_shapes=[
            pltpu.VMEM((parts, feat, 4 * SLOT), BF16),
            pltpu.VMEM((parts, feat, 4 * SLOT), BF16),
            pltpu.VMEM((4, 4, SLOT, D // 4), BF16),
            dma((parts,)), dma((parts,)), dma((4, 4)), dma((4, 4)),
        ],
        compiler_params=pltpu.CompilerParams(
            collective_id=2, has_side_effects=True, vmem_limit_bytes=48 * 1024 * 1024
        ),
        cost_estimate=pl.CostEstimate(flops=2_000_000_000, bytes_accessed=3_000_000, transcendentals=0),
        name="give",
    )(full_grad, place)


def per_device(tokens_in, out_grad, tenant, slot_of, steer_table, norm_gain, w_gate, w_up, w_down):
    feat_local = tokens_in.shape[1]
    token_count = tenant.shape[0]
    out_grad_t = out_grad.T
    gain_own = jnp.broadcast_to(norm_gain[:, None], (feat_local, 128))
    lines = slot_of.reshape(-1, 128).T
    halves = jnp.concatenate([lines // 256, lines % 256], axis=0).astype(BF16)
    tenant8 = jnp.broadcast_to(tenant[None, :], (8, token_count))
    residual, og_ext, wanted, place = fetch(
        tokens_in.T, jnp.concatenate([out_grad_t, gain_own], axis=1), tenant8, halves, steer_table
    )
    og_ext = og_ext.reshape(D, token_count + 128)
    full_grad = core(residual, out_grad_t, gain_own, og_ext, w_down, w_gate, w_up)
    rows = give(full_grad, place)
    rows = rows.transpose(1, 2, 0, 3).reshape(4 * SLOT, D)
    table_grad = lax.dot_general(wanted, rows, (((0,), (0,)), ((), ())), preferred_element_type=F32)
    return (full_grad.T, table_grad)


def solution(mesh):
    placed = (
        P("dp", "tensor"),
        P("dp", "tensor"),
        P("dp"),
        P(),
        P(("dp", "tensor"), None),
        P("tensor"),
        P(None, "tensor"),
        P(None, "tensor"),
        P("tensor", None),
    )
    return jax.shard_map(
        per_device,
        mesh=mesh,
        in_specs=placed,
        out_specs=(P("dp", "tensor"), P(("dp", "tensor"), None)),
        check_vma=False,
    )
```

```python
import functools

import jax
import jax.numpy as jnp
from jax import lax
from jax.experimental import pallas as pl
from jax.experimental.pallas import tpu as pltpu
from jax.sharding import PartitionSpec as P

D = 5120
F32 = jnp.float32
BF16 = jnp.bfloat16


CHUNKS = 3
SIDE = 4
HALF = 80
KB = 640
AG_P1 = 0
AG_P2 = 6
AG_SIB = 12
RS_SIB = 20
RS_R1 = 24
RS_R2 = 30
DOT_SIB = 36
DOT_X = 37
DOT_Z = 40
SLOTS = 43


def core_kernel(
    res_ref, og_own_ref, gain_own_ref, og_hbm, wd_hbm, wg_hbm, wu_hbm, wgt_hbm, wut_hbm,
    out_ref,
    x_all, wg, wu, wgt, wut, gain, og_buf, wd_buf, hid, y_buf, g_acc, u_acc, both, inv_s,
    part, sib_in, ra, rb, rc, rst, rsum, qa, qb, qc, qst,
    dp_, ds, dq, dxf, dxb, dxo, dr, dzf, dzb, dzo,
    ssem, rsem, lsem, hsem,
):
    ten = lax.axis_index("tensor")
    x = ten // 8
    z = lax.rem(ten // 2, 4)
    c = lax.rem(ten, 2)
    step = 1 - 2 * c
    xf, xb, xo = lax.rem(x + step + 4, 4), lax.rem(x - step + 4, 4), lax.rem(x + 2, 4)
    zf, zb, zo = lax.rem(z + step + 4, 4), lax.rem(z - step + 4, 4), lax.rem(z + 2, 4)

    def dev(xx, zz, cc):
        return {"tensor": (xx * 4 + zz) * 2 + cc}

    to_xf, to_xb = dev(xf, z, c), dev(xb, z, c)
    to_zf, to_zb = dev(x, zf, c), dev(x, zb, c)
    to_sib = dev(x, z, 1 - c)
    width = res_ref.shape[1]
    tok = width // CHUNKS
    rows = SIDE * 2 * 2 * HALF

    local = [
        pltpu.make_async_copy(wgt_hbm, wgt, lsem.at[0]),
        pltpu.make_async_copy(wut_hbm, wut, lsem.at[1]),
        pltpu.make_async_copy(wg_hbm, wg, lsem.at[2]),
        pltpu.make_async_copy(wu_hbm, wu, lsem.at[3]),
        pltpu.make_async_copy(og_hbm.at[:, pl.ds(width, 128)], gain, lsem.at[4]),
    ]

    def hidden_copies(j):
        return (
            pltpu.make_async_copy(og_hbm.at[pl.ds(j * KB, KB), pl.ds(0, width)], og_buf.at[j % 2], hsem.at[0, j % 2]),
            pltpu.make_async_copy(wd_hbm.at[:, pl.ds(j * KB, KB)], wd_buf.at[j % 2], hsem.at[1, j % 2]),
        )

    for copy in hidden_copies(0) + hidden_copies(1):
        copy.start()
    for copy in local:
        copy.start()

    for k in range(CHUNKS):
        for h in range(2):
            x_all[k, x, z, c, h] = res_ref[h * HALF:(h + 1) * HALF, k * tok:(k + 1) * tok]

    barrier = pltpu.get_barrier_semaphore()
    for where in (to_xf, to_xb, to_zf, to_zb, to_sib):
        pl.semaphore_signal(barrier, inc=1, device_id=where, device_id_type=pl.DeviceIdType.MESH)
    pl.semaphore_wait(barrier, 5)

    sent = []

    def move(src, dst, k, slot, where):
        copy = pltpu.make_async_remote_copy(
            src_ref=src, dst_ref=dst, send_sem=ssem.at[k, slot], recv_sem=rsem.at[k, slot],
            device_id=where, device_id_type=pl.DeviceIdType.MESH,
        )
        copy.start()
        sent.append(copy)

    def arrived(dst, k, slot, where):
        pltpu.make_async_remote_copy(
            src_ref=dst, dst_ref=dst, send_sem=ssem.at[k, slot], recv_sem=rsem.at[k, slot],
            device_id=where, device_id_type=pl.DeviceIdType.MESH,
        ).wait_recv()

    def one(k, xx, zz, h):
        return x_all.at[k, xx, zz, c, h]

    def line(k, h, at, cc):
        return x_all.at[k, at, :, cc, 0] if h == 0 else x_all.at[k, :, at, cc, 1]

    near_to = ((to_zf, to_zb), (to_xf, to_xb))
    far_to = ((to_xf, to_xb), (to_zf, to_zb))
    far_at = ((x, xb, xf, xo), (z, zb, zf, zo))

    def near(k, h, at):
        return one(k, x, at, 0) if h == 0 else one(k, at, z, 1)

    near_at = ((z, zb, zf, zo), (x, xb, xf, xo))

    def ag1(k):
        for h in range(2):
            own = one(k, x, z, h)
            move(own, own, k, AG_P1 + 3 * h, near_to[h][0])
            move(own, own, k, AG_P1 + 3 * h + 1, near_to[h][1])

    def ag2(k):
        for h in range(2):
            behind = near(k, h, near_at[h][1])
            arrived(behind, k, AG_P1 + 3 * h, near_to[h][1])
            move(behind, behind, k, AG_P1 + 3 * h + 2, near_to[h][0])

    def ag3(k):
        for h in range(2):
            arrived(near(k, h, near_at[h][2]), k, AG_P1 + 3 * h + 1, near_to[h][0])
            arrived(near(k, h, near_at[h][3]), k, AG_P1 + 3 * h + 2, near_to[h][1])
            own = line(k, h, far_at[h][0], c)
            move(own, own, k, AG_P2 + 3 * h, far_to[h][0])
            move(own, own, k, AG_P2 + 3 * h + 1, far_to[h][1])
            move(own, own, k, AG_SIB + 4 * h, to_sib)

    def ag4(k):
        for h in range(2):
            behind = line(k, h, far_at[h][1], c)
            arrived(behind, k, AG_P2 + 3 * h, far_to[h][1])
            move(behind, behind, k, AG_P2 + 3 * h + 2, far_to[h][0])
            move(behind, behind, k, AG_SIB + 4 * h + 1, to_sib)
        for h in range(2):
            ahead = line(k, h, far_at[h][2], c)
            arrived(ahead, k, AG_P2 + 3 * h + 1, far_to[h][0])
            move(ahead, ahead, k, AG_SIB + 4 * h + 2, to_sib)

    def ag5(k):
        for h in range(2):
            opposite = line(k, h, far_at[h][3], c)
            arrived(opposite, k, AG_P2 + 3 * h + 2, far_to[h][1])
            move(opposite, opposite, k, AG_SIB + 4 * h + 3, to_sib)

    def ag6(k):
        for h in range(2):
            at = far_at[h]
            for n, i in enumerate((0, 2, 1, 3)):
                arrived(line(k, h, at[i], 1 - c), k, AG_SIB + 4 * h + n, to_sib)

    def hidden(j):
        for copy in hidden_copies(j):
            copy.wait()
        part_sum = jnp.dot(wd_buf[j % 2], og_buf[j % 2], preferred_element_type=F32)
        if j == 0:
            hid[...] = part_sum
        else:
            hid[...] += part_sum
        if j + 2 < D // KB:
            for copy in hidden_copies(j + 2):
                copy.start()

    def gates(k):
        g_acc[...] = jnp.zeros_like(g_acc)
        u_acc[...] = jnp.zeros_like(u_acc)

        def body(i, squares):
            at = pl.multiple_of(i * rows, rows)
            wide = x_all[k, i].reshape(rows, tok).astype(F32)
            scale = gain[pl.ds(at, rows), :].astype(F32)
            scale = jnp.concatenate([scale] * (tok // 128), axis=1)
            y_buf[...] = (wide * scale).astype(BF16)
            g_acc[...] += jnp.dot(wgt[:, pl.ds(at, rows)], y_buf[...], preferred_element_type=F32)
            u_acc[...] += jnp.dot(wut[:, pl.ds(at, rows)], y_buf[...], preferred_element_type=F32)
            return squares + jnp.sum(wide * wide, axis=0, keepdims=True)

        squares = lax.fori_loop(0, SIDE, body, jnp.zeros((1, tok), F32))
        inverse = lax.rsqrt(squares / D + 1e-06)
        inv_s[k] = jnp.broadcast_to(inverse, (8, tok))
        gate_out = g_acc[...] * inverse
        up_out = u_acc[...] * inverse
        hidden_grad = hid[:, k * tok:(k + 1) * tok]
        sigma = jax.nn.sigmoid(gate_out)
        gate_grad = (hidden_grad * up_out * (sigma * (1.0 + gate_out * (1.0 - sigma)))).astype(BF16)
        up_grad = (hidden_grad * (gate_out * sigma)).astype(BF16)
        half = gate_grad.shape[0]
        both[0:half] = gate_grad
        both[half:2 * half] = up_grad
        dots = jnp.sum(gate_grad.astype(F32) * gate_out + up_grad.astype(F32) * up_out, axis=0, keepdims=True)
        dp_[k] = jnp.broadcast_to(dots, (8, tok))
        move(dp_.at[k], dq.at[k], k, DOT_SIB, to_sib)

    def last(k):
        half = both.shape[0] // 2

        for i in range(SIDE):
            at = i * rows
            term = jnp.dot(wg[at:at + rows, :], both[0:half], preferred_element_type=F32)
            term = term + jnp.dot(wu[at:at + rows, :], both[half:2 * half], preferred_element_type=F32)
            part[k, i] = term.astype(BF16).reshape(SIDE, 2, 2, HALF, tok)
            move(part.at[k, i, :, 1 - c], sib_in.at[k, i], k, RS_SIB + i, to_sib)

    def add(*refs_):
        total = refs_[0].astype(F32)
        for other in refs_[1:]:
            total = total + other.astype(F32)
        return total

    def chip_line(k, h, at):
        return part.at[k, at, :, c, 0] if h == 0 else part.at[k, :, at, c, 1]

    def rs0(k):
        for i in range(SIDE):
            arrived(sib_in.at[k, i], k, RS_SIB + i, to_sib)
            part[k, i, :, c] = add(part[k, i, :, c], sib_in[k, i]).astype(BF16)
        for h in range(2):
            move(chip_line(k, h, far_at[h][3]), ra.at[k, h], k, RS_R1 + 3 * h, far_to[h][0])
        for h in range(2):
            move(chip_line(k, h, far_at[h][1]), rb.at[k, h], k, RS_R1 + 3 * h + 1, far_to[h][1])
        arrived(dq.at[k], k, DOT_SIB, to_sib)
        ds[k] = dp_[k] + dq[k]

    def rs0b(k):
        move(ds.at[k], dxf.at[k], k, DOT_X, to_xf)
        move(ds.at[k], dxb.at[k], k, DOT_X + 1, to_xb)

    def rs1(k):
        for h in range(2):
            arrived(ra.at[k, h], k, RS_R1 + 3 * h, far_to[h][1])
            rst[k, h] = add(ra[k, h], chip_line(k, h, far_at[h][2])[...]).astype(BF16)
            move(rst.at[k, h], rc.at[k, h], k, RS_R1 + 3 * h + 2, far_to[h][0])
        arrived(dxf.at[k], k, DOT_X, to_xb)
        move(dxf.at[k], dxo.at[k], k, DOT_X + 2, to_xf)

    def rs2(k):
        for h in range(2):
            arrived(rb.at[k, h], k, RS_R1 + 3 * h + 1, far_to[h][0])
            arrived(rc.at[k, h], k, RS_R1 + 3 * h + 2, far_to[h][1])
            rsum[k, h] = add(chip_line(k, h, far_at[h][0])[...], rb[k, h], rc[k, h]).astype(BF16)
            move(rsum.at[k, h, near_at[h][3]], qa.at[k, h], k, RS_R2 + 3 * h, near_to[h][0])
            move(rsum.at[k, h, near_at[h][1]], qb.at[k, h], k, RS_R2 + 3 * h + 1, near_to[h][1])
        arrived(dxb.at[k], k, DOT_X + 1, to_xf)
        arrived(dxo.at[k], k, DOT_X + 2, to_xb)
        dr[k] = ds[k] + dxf[k] + dxb[k] + dxo[k]
        move(dr.at[k], dzf.at[k], k, DOT_Z, to_zf)
        move(dr.at[k], dzb.at[k], k, DOT_Z + 1, to_zb)

    def rs3(k):
        for h in range(2):
            arrived(qa.at[k, h], k, RS_R2 + 3 * h, near_to[h][1])
            qst[k, h] = add(qa[k, h], rsum[k, h, near_at[h][2]]).astype(BF16)
            move(qst.at[k, h], qc.at[k, h], k, RS_R2 + 3 * h + 2, near_to[h][0])
        arrived(dzf.at[k], k, DOT_Z, to_zb)
        move(dzf.at[k], dzo.at[k], k, DOT_Z + 2, to_zf)

    def rs4(k):
        arrived(dzb.at[k], k, DOT_Z + 1, to_zf)
        arrived(dzo.at[k], k, DOT_Z + 2, to_zb)
        dots = (dr[k] + dzf[k] + dzb[k] + dzo[k])[0:1]
        inverse = inv_s[k][0:1]
        pull = dots * inverse * inverse / D
        for h in range(2):
            arrived(qb.at[k, h], k, RS_R2 + 3 * h + 1, near_to[h][0])
            arrived(qc.at[k, h], k, RS_R2 + 3 * h + 2, near_to[h][1])
            norm_grad = add(rsum[k, h, near_at[h][0]], qb[k, h], qc[k, h])
            span = slice(h * HALF, (h + 1) * HALF)
            cols = slice(k * tok, (k + 1) * tok)
            full = og_own_ref[span, cols].astype(F32) + gain_own_ref[span, 0:1].astype(F32) * inverse * norm_grad
            full = full - res_ref[span, cols].astype(F32) * pull
            out_ref[span, cols] = full.astype(BF16)

    def wait_local(*which):
        for n in which:
            local[n].wait()

    for k in range(CHUNKS):
        ag1(k)
    hidden(0)
    ag2(0)
    hidden(1)
    ag3(0)
    ag2(1)
    hidden(2)
    ag3(1)
    ag2(2)
    hidden(3)
    ag4(0)
    hidden(4)
    ag3(2)
    hidden(5)
    ag5(0)
    hidden(6)
    ag4(1)
    hidden(7)
    wait_local(4, 0, 1)
    ag6(0)
    gates(0)
    ag5(1)
    ag4(2)
    wait_local(2, 3)
    last(0)
    ag6(1)
    gates(1)
    rs0(0)
    rs0b(0)
    ag5(2)
    last(1)
    rs1(0)
    ag6(2)
    gates(2)
    rs2(0)
    rs0(1)
    rs0b(1)
    last(2)
    rs3(0)
    rs1(1)
    rs4(0)
    rs0(2)
    rs0b(2)
    rs2(1)
    rs3(1)
    rs1(2)
    rs4(1)
    rs2(2)
    rs3(2)
    rs4(2)
    for copy in sent:
        copy.wait_send()


def core(residual, out_grad_t, gain_own, og_ext, w_down, w_gate, w_up, w_gate_t, w_up_t):
    width = residual.shape[1]
    tok = width // CHUNKS
    hid = w_gate.shape[1]
    vm = pl.BlockSpec(memory_space=pltpu.VMEM)
    hbm = pl.BlockSpec(memory_space=pl.ANY)

    def bf(*shape):
        return pltpu.VMEM(shape, BF16)

    def fl(*shape):
        return pltpu.VMEM(shape, F32)

    rows = SIDE * 2 * 2 * HALF
    return pl.pallas_call(
        core_kernel,
        out_shape=jax.ShapeDtypeStruct(residual.shape, BF16),
        in_specs=[vm] * 3 + [hbm] * 6,
        out_specs=vm,
        scratch_shapes=[
            bf(CHUNKS, SIDE, SIDE, 2, 2, HALF, tok),
            bf(D, hid), bf(D, hid), bf(hid, D), bf(hid, D),
            bf(D, 128),
            bf(2, KB, width), bf(2, hid, KB),
            fl(hid, width),
            bf(rows, tok), fl(hid, tok), fl(hid, tok), bf(2 * hid, tok), fl(CHUNKS, 8, tok),
            bf(CHUNKS, SIDE, SIDE, 2, 2, HALF, tok), bf(CHUNKS, SIDE, SIDE, 2, HALF, tok),
        ]
        + [bf(CHUNKS, 2, SIDE, HALF, tok)] * 5
        + [bf(CHUNKS, 2, HALF, tok)] * 4
        + [fl(CHUNKS, 8, tok)] * 10
        + [
            pltpu.SemaphoreType.DMA((CHUNKS, SLOTS)),
            pltpu.SemaphoreType.DMA((CHUNKS, SLOTS)),
            pltpu.SemaphoreType.DMA((5,)),
            pltpu.SemaphoreType.DMA((2, 2)),
        ],
        compiler_params=pltpu.CompilerParams(
            collective_id=0, has_side_effects=True, vmem_limit_bytes=60 * 1024 * 1024
        ),
        cost_estimate=pl.CostEstimate(flops=10 * D * hid * width, bytes_accessed=40_000_000, transcendentals=0),
        name="core",
    )(residual, out_grad_t, gain_own, og_ext, w_down, w_gate, w_up, w_gate_t, w_up_t)


MESH = pl.DeviceIdType.MESH
SLOT = 32
SPANS = ((0, 512), (512, 384))


def nt(a, b):
    return lax.dot_general(a, b, (((1,), (1,)), ((), ())), preferred_element_type=F32)


def fetch_kernel(
    tok_ref, og_ref, ten_ref, halves_ref, table_ref, wg_hbm, wu_hbm,
    res_ref, og_out, wanted_ref, place_ref, wgt_hbm, wut_hbm,
    tbuf, earlier, rows_s, rows_r, turned, landed, acc, w_buf, wt_buf,
    tsend, trecv, ysend, yrecv, psend, precv, gsend, grecv, lsem,
):
    d = lax.axis_index("dp")
    t = lax.axis_index("tensor")
    me = d * 32 + t
    x = t // 8
    z = lax.rem(t // 2, 4)
    c = lax.rem(t, 2)
    step = 1 - 2 * c
    xf, xb, xo = lax.rem(x + step + 4, 4), lax.rem(x - step + 4, 4), lax.rem(x + 2, 4)
    zf, zb, zo = lax.rem(z + step + 4, 4), lax.rem(z - step + 4, 4), lax.rem(z + 2, 4)

    def dev(xx, zz, cc):
        return {"dp": d, "tensor": (xx * 4 + zz) * 2 + cc}

    to_xf, to_xb = dev(xf, z, c), dev(xb, z, c)
    to_zf, to_zb = dev(x, zf, c), dev(x, zb, c)
    to_sib = dev(x, z, 1 - c)
    width = tok_ref.shape[1]
    feat = tok_ref.shape[0]
    parts = D // feat

    own_copies = [
        pltpu.make_async_copy(og_ref.at[pl.ds(h * HALF, HALF)], og_out.at[x, z, c, h], lsem.at[h]) for h in range(2)
    ]
    for copy in own_copies:
        copy.start()
    w_in = [pltpu.make_async_copy(src, w_buf.at[n], lsem.at[2 + n]) for n, src in enumerate((wg_hbm, wu_hbm))]
    w_out = [pltpu.make_async_copy(wt_buf.at[n], dst, lsem.at[4 + n]) for n, dst in enumerate((wgt_hbm, wut_hbm))]
    for copy in w_in:
        copy.start()
    barrier = pltpu.get_barrier_semaphore()

    def greet(o, carry):
        pl.semaphore_signal(
            barrier, inc=1, device_id={"dp": d, "tensor": lax.rem(t + o, parts)}, device_id_type=MESH
        )
        return carry

    lax.fori_loop(1, parts, greet, 0)
    for o in (1, 2, 3):
        pl.semaphore_signal(barrier, inc=1, device_id={"dp": lax.rem(d + o, 4), "tensor": t}, device_id_type=MESH)
    pl.semaphore_wait(barrier, parts - 1 + 3)

    sent = []

    def send(src, dst, ssem, rsem, where):
        copy = pltpu.make_async_remote_copy(
            src_ref=src, dst_ref=dst, send_sem=ssem, recv_sem=rsem, device_id=where, device_id_type=MESH
        )
        copy.start()
        sent.append(copy)

    def got(dst, ssem, rsem, where):
        pltpu.make_async_remote_copy(
            src_ref=dst, dst_ref=dst, send_sem=ssem, recv_sem=rsem, device_id=where, device_id_type=MESH
        ).wait_recv()

    for o in (1, 3, 2):
        there = lax.rem(d + o, 4)
        send(ten_ref, tbuf.at[d], tsend.at[there], trecv.at[d], {"dp": there, "tensor": t})

    near_to = ((to_zf, to_zb), (to_xf, to_xb))
    far_to = ((to_xf, to_xb), (to_zf, to_zb))
    near_at = ((z, zb, zf, zo), (x, xb, xf, xo))
    far_at = ((x, xb, xf, xo), (z, zb, zf, zo))

    def lanes(k):
        return pl.ds(SPANS[k][0], SPANS[k][1])

    def near(k, h, at):
        return og_out.at[x, at, c, 0, :, lanes(k)] if h == 0 else og_out.at[at, z, c, 1, :, lanes(k)]

    def line(k, h, at, cc):
        return og_out.at[at, :, cc, 0, :, lanes(k)] if h == 0 else og_out.at[:, at, cc, 1, :, lanes(k)]

    def move(src, dst, k, slot, where):
        send(src, dst, gsend.at[k, slot], grecv.at[k, slot], where)

    def arrived(dst, k, slot, where):
        got(dst, gsend.at[k, slot], grecv.at[k, slot], where)

    def ag1(k):
        for h in range(2):
            own = near(k, h, near_at[h][0])
            src = og_ref.at[pl.ds(h * HALF, HALF), lanes(k)]
            move(src, own, k, AG_P1 + 3 * h, near_to[h][0])
            move(src, own, k, AG_P1 + 3 * h + 1, near_to[h][1])

    def ag2(k):
        for h in range(2):
            behind = near(k, h, near_at[h][1])
            arrived(behind, k, AG_P1 + 3 * h, near_to[h][1])
            move(behind, behind, k, AG_P1 + 3 * h + 2, near_to[h][0])

    def ag3(k):
        for h in range(2):
            arrived(near(k, h, near_at[h][2]), k, AG_P1 + 3 * h + 1, near_to[h][0])
            arrived(near(k, h, near_at[h][3]), k, AG_P1 + 3 * h + 2, near_to[h][1])
            own = line(k, h, far_at[h][0], c)
            move(own, own, k, AG_P2 + 3 * h, far_to[h][0])
            move(own, own, k, AG_P2 + 3 * h + 1, far_to[h][1])
            move(own, own, k, AG_SIB + 4 * h, to_sib)

    def ag4(k):
        for h in range(2):
            behind = line(k, h, far_at[h][1], c)
            arrived(behind, k, AG_P2 + 3 * h, far_to[h][1])
            move(behind, behind, k, AG_P2 + 3 * h + 2, far_to[h][0])
            move(behind, behind, k, AG_SIB + 4 * h + 1, to_sib)
        for h in range(2):
            ahead = line(k, h, far_at[h][2], c)
            arrived(ahead, k, AG_P2 + 3 * h + 1, far_to[h][0])
            move(ahead, ahead, k, AG_SIB + 4 * h + 2, to_sib)

    def ag5(k):
        for h in range(2):
            opposite = line(k, h, far_at[h][3], c)
            arrived(opposite, k, AG_P2 + 3 * h + 2, far_to[h][1])
            move(opposite, opposite, k, AG_SIB + 4 * h + 3, to_sib)

    def ag6(k):
        for h in range(2):
            for n, i in enumerate((0, 2, 1, 3)):
                arrived(line(k, h, far_at[h][i], 1 - c), k, AG_SIB + 4 * h + n, to_sib)

    ag1(0)
    ag1(1)

    lines = halves_ref.shape[1]
    earlier[...] = (
        lax.broadcasted_iota(jnp.int32, (width, width), 0) < lax.broadcasted_iota(jnp.int32, (width, width), 1)
    ).astype(F32).astype(BF16)

    def hot(index, size):
        return (lax.broadcasted_iota(jnp.int32, (size, width), 0) == index).astype(F32)

    def look_up(tenant):
        picked = jnp.dot(halves_ref[...], hot(tenant // 128, lines).astype(BF16), preferred_element_type=F32)
        lane = hot(lax.rem(tenant, 128), 128)
        owner = jnp.sum(lane * picked[:128], axis=0, keepdims=True).astype(jnp.int32)
        row = jnp.sum(lane * picked[128:], axis=0, keepdims=True).astype(jnp.int32)
        return owner, row

    def ranks(matches):
        before = jnp.dot(matches.astype(BF16), earlier[...], preferred_element_type=F32)
        return jnp.sum(matches * before, axis=0, keepdims=True).astype(jnp.int32)

    owner, row = look_up(ten_ref[0:1])
    rank = ranks(hot(owner, 128))
    place = lax.rem(owner, 32) * 128 + owner // 32 * SLOT + rank
    place_ref[...] = jnp.broadcast_to(place, place_ref.shape)
    ag2(0)
    ag2(1)

    tbuf[d] = ten_ref[...]
    for o in (1, 3, 2):
        there = lax.rem(d + o, 4)
        got(tbuf.at[there], tsend.at[there], trecv.at[there], {"dp": there, "tensor": t})
    for g in range(4):
        owner, row = look_up(tbuf[g, 0:1])
        mine = (owner == me).astype(F32)
        mine8 = jnp.broadcast_to(mine, (8, width))
        before = jnp.dot(mine8.astype(BF16), earlier[...], preferred_element_type=F32)[0:1]
        slot = jnp.where(mine > 0, before.astype(jnp.int32), -1)
        wanted = nt(hot(slot, SLOT).astype(BF16), hot(row, table_ref.shape[0]).astype(BF16)).astype(BF16)
        wanted_ref[g * SLOT:(g + 1) * SLOT] = wanted

    quarter = D // 4

    def y_copy(q, there, at):
        return pltpu.make_async_remote_copy(
            src_ref=rows_s.at[q, there], dst_ref=rows_r.at[q, at], send_sem=ysend.at[q, there], recv_sem=yrecv.at[q, at],
            device_id={"dp": there, "tensor": t}, device_id_type=MESH,
        )

    others = tuple(lax.rem(d + o, 4) for o in (1, 3, 2))
    order = (x, lax.rem(x + 1, 4), lax.rem(x + 3, 4), xo)

    def pick(q):
        cols = pl.ds(pl.multiple_of(q * quarter, quarter), quarter)
        picked = jnp.dot(wanted_ref[...], table_ref[:, cols], preferred_element_type=F32)
        rows_s[q] = picked.astype(BF16).reshape(4, SLOT, quarter)
        for there in others:
            y_copy(q, there, d).start()
        rows_r[q, d] = rows_s[q, d]

    for q in order:
        pick(q)
    for copy in own_copies:
        copy.wait()
    ag3(0)
    ag3(1)

    def turn_weight(n):
        w_in[n].wait()
        wide = 640

        def body(i, carry):
            at = pl.multiple_of(i * wide, wide)
            wt_buf[n, :, pl.ds(at, wide)] = w_buf[n, pl.ds(at, wide), :].T
            return carry

        lax.fori_loop(0, D // wide, body, 0)
        w_out[n].start()

    def plane_copy(there):
        return pltpu.make_async_remote_copy(
            src_ref=turned.at[there], dst_ref=landed.at[t], send_sem=psend.at[there], recv_sem=precv.at[t],
            device_id={"dp": d, "tensor": there}, device_id_type=MESH,
        )

    row = parts // 4

    def pass_on(n):
        q = order[n]
        for there in others:
            pltpu.make_async_remote_copy(
                src_ref=rows_r.at[q, there], dst_ref=rows_r.at[q, there],
                send_sem=ysend.at[q, there], recv_sem=yrecv.at[q, there],
                device_id={"dp": there, "tensor": t}, device_id_type=MESH,
            ).wait_recv()
        turned[pl.ds(q * row, row)] = rows_r[q].reshape(4 * SLOT, quarter).T.reshape(row, feat, 4 * SLOT)

        def scatter(i, carry):
            plane_copy(q * row + lax.rem(lax.rem(t, row) + i, row)).start()
            return carry

        lax.fori_loop(1 if n == 0 else 0, row, scatter, 0)
        if n == 0:
            landed[t] = turned[t]

    turn_weight(0)
    pass_on(0)
    ag4(0)
    pass_on(1)
    pass_on(2)
    pass_on(3)
    acc[...] = tok_ref[...].astype(F32)
    turn_weight(1)
    ag4(1)
    ag5(0)

    def arrive(src):
        @pl.when(src != t)
        def _():
            pltpu.make_async_remote_copy(
                src_ref=landed.at[src], dst_ref=landed.at[src], send_sem=psend.at[src], recv_sem=precv.at[src],
                device_id={"dp": d, "tensor": src}, device_id_type=MESH,
            ).wait_recv()

    def gather(q):
        def body(i, carry):
            pair = q * (row // 2) + i
            arrive(2 * pair)
            arrive(2 * pair + 1)
            sel = (lax.broadcasted_iota(jnp.int32, (256, width), 0) + pair * 256 == place).astype(F32).astype(BF16)
            both = jnp.concatenate([landed[2 * pair], landed[2 * pair + 1]], axis=1)
            acc[...] += jnp.dot(both, sel, preferred_element_type=F32)
            return carry

        lax.fori_loop(0, row // 2, body, 0)

    gather(x)
    ag5(1)
    gather(order[2])
    gather(order[1])
    ag6(0)
    gather(xo)
    res_ref[...] = acc[...].astype(BF16)
    ag6(1)

    def drain(o, carry):
        plane_copy(lax.rem(t + o, parts)).wait_send()
        return carry

    lax.fori_loop(1, parts, drain, 0)
    for q in range(4):
        for there in others:
            y_copy(q, there, d).wait_send()
    for copy in sent:
        copy.wait_send()
    for copy in w_out:
        copy.wait()


def fetch(tokens_t, og_ext, tenant8, halves, table, w_gate, w_up):
    feat, width = tokens_t.shape
    parts = D // feat
    vm = pl.BlockSpec(memory_space=pltpu.VMEM)
    hbm = pl.BlockSpec(memory_space=pl.ANY)
    dma = pltpu.SemaphoreType.DMA
    return pl.pallas_call(
        fetch_kernel,
        out_shape=(
            jax.ShapeDtypeStruct((feat, width), BF16),
            jax.ShapeDtypeStruct((SIDE, SIDE, 2, 2, HALF, og_ext.shape[1]), BF16),
            jax.ShapeDtypeStruct((4 * SLOT, table.shape[0]), BF16),
            jax.ShapeDtypeStruct((8, width), jnp.int32),
            jax.ShapeDtypeStruct(w_gate.shape[::-1], BF16),
            jax.ShapeDtypeStruct(w_up.shape[::-1], BF16),
        ),
        in_specs=[vm] * 5 + [hbm] * 2,
        out_specs=(vm, hbm, vm, vm, hbm, hbm),
        scratch_shapes=[
            pltpu.VMEM((4, 8, width), jnp.int32),
            pltpu.VMEM((width, width), BF16),
            pltpu.VMEM((4, 4, SLOT, D // 4), BF16),
            pltpu.VMEM((4, 4, SLOT, D // 4), BF16),
            pltpu.VMEM((parts, feat, 4 * SLOT), BF16),
            pltpu.VMEM((parts, feat, 4 * SLOT), BF16),
            pltpu.VMEM((feat, width), F32),
            pltpu.VMEM((2,) + w_gate.shape, BF16),
            pltpu.VMEM((2,) + w_gate.shape[::-1], BF16),
            dma((4,)), dma((4,)), dma((4, 4)), dma((4, 4)), dma((parts,)), dma((parts,)),
            dma((len(SPANS), RS_SIB)), dma((len(SPANS), RS_SIB)), dma((6,)),
        ],
        compiler_params=pltpu.CompilerParams(
            collective_id=1, has_side_effects=True, vmem_limit_bytes=48 * 1024 * 1024
        ),
        cost_estimate=pl.CostEstimate(flops=4_000_000_000, bytes_accessed=20_000_000, transcendentals=0),
        name="fetch",
    )(tokens_t, og_ext, tenant8, halves, table, w_gate, w_up)


def give_kernel(full_ref, place_ref, rows_r, leaving, landed, rows_s, psend, precv, ysend, yrecv):
    d = lax.axis_index("dp")
    t = lax.axis_index("tensor")
    feat, width = full_ref.shape
    parts = D // feat
    barrier = pltpu.get_barrier_semaphore()

    def greet(o, carry):
        pl.semaphore_signal(
            barrier, inc=1, device_id={"dp": d, "tensor": lax.rem(t + o, parts)}, device_id_type=MESH
        )
        return carry

    lax.fori_loop(1, parts, greet, 0)
    for o in (1, 2, 3):
        pl.semaphore_signal(barrier, inc=1, device_id={"dp": lax.rem(d + o, 4), "tensor": t}, device_id_type=MESH)

    place = place_ref[0:1]
    pl.semaphore_wait(barrier, parts - 1 + 3)

    def plane_copy(there, at):
        return pltpu.make_async_remote_copy(
            src_ref=leaving.at[there], dst_ref=landed.at[at], send_sem=psend.at[there], recv_sem=precv.at[at],
            device_id={"dp": d, "tensor": there}, device_id_type=MESH,
        )

    def pack(pair):
        sel = (lax.broadcasted_iota(jnp.int32, (256, width), 0) + pair * 256 == place).astype(F32).astype(BF16)
        packed = nt(full_ref[...], sel).astype(BF16)
        for half in range(2):
            there = 2 * pair + half
            leaving[there] = packed[:, 128 * half:128 * half + 128]

            @pl.when(there != t)
            def _():
                plane_copy(there, t).start()

    quad = parts // 8
    x = t // 8

    def own_row(i, carry):
        pack(x * quad + lax.rem(lax.rem(t // 2, quad) + i, quad))
        return carry

    def side_rows(i, carry):
        at = lax.rem(lax.rem(t // 2, quad) + i, quad)
        pack(lax.rem(x + 1, 4) * quad + at)
        pack(lax.rem(x + 3, 4) * quad + at)
        return carry

    def far_row(i, carry):
        pack(lax.rem(x + 2, 4) * quad + lax.rem(lax.rem(t // 2, quad) + i, quad))
        return carry

    lax.fori_loop(0, quad, own_row, 0)
    landed[t] = leaving[t]
    lax.fori_loop(0, quad, side_rows, 0)
    lax.fori_loop(0, quad, far_row, 0)

    group = 8

    def y_copy(q, there):
        return pltpu.make_async_remote_copy(
            src_ref=rows_s.at[q, there], dst_ref=rows_r.at[q, d], send_sem=ysend.at[q, there], recv_sem=yrecv.at[q, d],
            device_id={"dp": there, "tensor": t}, device_id_type=MESH,
        )

    def arrive(src):
        @pl.when(src != t)
        def _():
            pltpu.make_async_remote_copy(
                src_ref=landed.at[src], dst_ref=landed.at[src], send_sem=psend.at[src], recv_sem=precv.at[src],
                device_id={"dp": d, "tensor": src}, device_id_type=MESH,
            ).wait_recv()

    for q in (x, lax.rem(x + 3, 4), lax.rem(x + 1, 4), lax.rem(x + 2, 4)):

        def take(i, inner):
            arrive(q * group + i)
            return inner

        lax.fori_loop(0, group, take, 0)
        block = landed[pl.ds(q * group, group)].reshape(group * feat, 4 * SLOT)
        rows_s[q] = block.T.reshape(4, SLOT, group * feat)
        for o in (1, 3, 2):
            y_copy(q, lax.rem(d + o, 4)).start()
        rows_r[q, d] = rows_s[q, d]

    def finish(q, carry):
        for o in (1, 3, 2):
            there = lax.rem(d + o, 4)
            y_copy(q, there).wait_send()
            pltpu.make_async_remote_copy(
                src_ref=rows_r.at[q, there], dst_ref=rows_r.at[q, there],
                send_sem=ysend.at[q, there], recv_sem=yrecv.at[q, there],
                device_id={"dp": there, "tensor": t}, device_id_type=MESH,
            ).wait_recv()
        return carry

    lax.fori_loop(0, 4, finish, 0)

    def drain(o, carry):
        plane_copy(lax.rem(t + o, parts), t).wait_send()
        return carry

    lax.fori_loop(1, parts, drain, 0)


def give(full_grad, place):
    feat, width = full_grad.shape
    parts = D // feat
    vm = pl.BlockSpec(memory_space=pltpu.VMEM)
    dma = pltpu.SemaphoreType.DMA
    return pl.pallas_call(
        give_kernel,
        out_shape=jax.ShapeDtypeStruct((4, 4, SLOT, D // 4), BF16),
        in_specs=[vm] * 2,
        out_specs=vm,
        scratch_shapes=[
            pltpu.VMEM((parts, feat, 4 * SLOT), BF16),
            pltpu.VMEM((parts, feat, 4 * SLOT), BF16),
            pltpu.VMEM((4, 4, SLOT, D // 4), BF16),
            dma((parts,)), dma((parts,)), dma((4, 4)), dma((4, 4)),
        ],
        compiler_params=pltpu.CompilerParams(
            collective_id=2, has_side_effects=True, vmem_limit_bytes=48 * 1024 * 1024
        ),
        cost_estimate=pl.CostEstimate(flops=2_000_000_000, bytes_accessed=3_000_000, transcendentals=0),
        name="give",
    )(full_grad, place)


def per_device(tokens_in, out_grad, tenant, slot_of, steer_table, norm_gain, w_gate, w_up, w_down):
    feat_local = tokens_in.shape[1]
    token_count = tenant.shape[0]
    out_grad_t = out_grad.T
    gain_own = jnp.broadcast_to(norm_gain[:, None], (feat_local, 128))
    lines = slot_of.reshape(-1, 128).T
    halves = jnp.concatenate([lines // 256, lines % 256], axis=0).astype(BF16)
    tenant8 = jnp.broadcast_to(tenant[None, :], (8, token_count))
    residual, og_ext, wanted, place, w_gate_t, w_up_t = fetch(
        tokens_in.T, jnp.concatenate([out_grad_t, gain_own], axis=1), tenant8, halves, steer_table, w_gate, w_up
    )
    og_ext = og_ext.reshape(D, token_count + 128)
    full_grad = core(residual, out_grad_t, gain_own, og_ext, w_down, w_gate, w_up, w_gate_t, w_up_t)
    rows = give(full_grad, place)
    rows = rows.transpose(1, 2, 0, 3).reshape(4 * SLOT, D)
    table_grad = lax.dot_general(wanted, rows, (((0,), (0,)), ((), ())), preferred_element_type=F32)
    return (full_grad.T, table_grad)


def solution(mesh):
    placed = (
        P("dp", "tensor"),
        P("dp", "tensor"),
        P("dp"),
        P(),
        P(("dp", "tensor"), None),
        P("tensor"),
        P(None, "tensor"),
        P(None, "tensor"),
        P("tensor", None),
    )
    return jax.shard_map(
        per_device,
        mesh=mesh,
        in_specs=placed,
        out_specs=(P("dp", "tensor"), P(("dp", "tensor"), None)),
        check_vma=False,
    )
```

```python
import functools

import jax
import jax.numpy as jnp
from jax import lax
from jax.experimental import pallas as pl
from jax.experimental.pallas import tpu as pltpu
from jax.sharding import PartitionSpec as P

D = 5120
F32 = jnp.float32
BF16 = jnp.bfloat16


CHUNKS = 3
SIDE = 4
HALF = 80
KB = 640
AG_P1 = 0
AG_P2 = 6
AG_SIB = 12
RS_SIB = 20
RS_R1 = 24
RS_R2 = 30
DOT_SIB = 36
DOT_X = 37
DOT_Z = 40
SLOTS = 43


def core_kernel(
    res_ref, og_own_ref, gain_own_ref, og_hbm, wd_hbm, wg_hbm, wu_hbm, wgt_hbm, wut_hbm,
    out_ref,
    x_all, w_out, w_in, gain, og_buf, wd_buf, hid, y_buf, acc, squares, both, inv_s,
    part, sib_in, ra, rb, rc, rst, rsum, qa, qb, qc,
    dp_, ds, dq, dxf, dxb, dxo, dr, dzf, dzb, dzo,
    ssem, rsem, lsem, hsem,
):
    ten = lax.axis_index("tensor")
    x = ten // 8
    z = lax.rem(ten // 2, 4)
    c = lax.rem(ten, 2)
    step = 1 - 2 * c
    xf, xb, xo = lax.rem(x + step + 4, 4), lax.rem(x - step + 4, 4), lax.rem(x + 2, 4)
    zf, zb, zo = lax.rem(z + step + 4, 4), lax.rem(z - step + 4, 4), lax.rem(z + 2, 4)

    def dev(xx, zz, cc):
        return {"tensor": (xx * 4 + zz) * 2 + cc}

    to_xf, to_xb = dev(xf, z, c), dev(xb, z, c)
    to_zf, to_zb = dev(x, zf, c), dev(x, zb, c)
    to_xo, to_zo = dev(xo, z, c), dev(x, zo, c)
    to_sib = dev(x, z, 1 - c)
    width = res_ref.shape[1]
    tok = width // CHUNKS
    rows = SIDE * 2 * 2 * HALF

    half = wg_hbm.shape[1]
    local = [
        pltpu.make_async_copy(wgt_hbm, w_in.at[pl.ds(0, half)], lsem.at[0]),
        pltpu.make_async_copy(wut_hbm, w_in.at[pl.ds(half, half)], lsem.at[1]),
        pltpu.make_async_copy(wg_hbm, w_out.at[:, pl.ds(0, half)], lsem.at[2]),
        pltpu.make_async_copy(wu_hbm, w_out.at[:, pl.ds(half, half)], lsem.at[3]),
        pltpu.make_async_copy(og_hbm.at[:, pl.ds(width, 128)], gain, lsem.at[4]),
    ]

    def hidden_copies(j):
        return (
            pltpu.make_async_copy(og_hbm.at[pl.ds(j * KB, KB), pl.ds(0, width)], og_buf.at[j % 2], hsem.at[0, j % 2]),
            pltpu.make_async_copy(wd_hbm.at[:, pl.ds(j * KB, KB)], wd_buf.at[j % 2], hsem.at[1, j % 2]),
        )

    for copy in hidden_copies(0) + hidden_copies(1):
        copy.start()
    local[4].start()

    for k in range(CHUNKS):
        for h in range(2):
            x_all[k, x, z, c, h] = res_ref[h * HALF:(h + 1) * HALF, k * tok:(k + 1) * tok]

    barrier = pltpu.get_barrier_semaphore()
    for where in (to_xf, to_xb, to_xo, to_zf, to_zb, to_zo, to_sib):
        pl.semaphore_signal(barrier, inc=1, device_id=where, device_id_type=pl.DeviceIdType.MESH)
    pl.semaphore_wait(barrier, 7)

    sent = []

    def move(src, dst, k, slot, where):
        copy = pltpu.make_async_remote_copy(
            src_ref=src, dst_ref=dst, send_sem=ssem.at[k, slot], recv_sem=rsem.at[k, slot],
            device_id=where, device_id_type=pl.DeviceIdType.MESH,
        )
        copy.start()
        sent.append(copy)

    def arrived(dst, k, slot, where):
        pltpu.make_async_remote_copy(
            src_ref=dst, dst_ref=dst, send_sem=ssem.at[k, slot], recv_sem=rsem.at[k, slot],
            device_id=where, device_id_type=pl.DeviceIdType.MESH,
        ).wait_recv()

    def one(k, xx, zz, h):
        return x_all.at[k, xx, zz, c, h]

    def line(k, h, at, cc):
        return x_all.at[k, at, :, cc, 0] if h == 0 else x_all.at[k, :, at, cc, 1]

    near_to = ((to_zf, to_zb, to_zo), (to_xf, to_xb, to_xo))
    far_to = ((to_xf, to_xb), (to_zf, to_zb))
    far_at = ((x, xb, xf, xo), (z, zb, zf, zo))

    def near(k, h, at):
        return one(k, x, at, 0) if h == 0 else one(k, at, z, 1)

    near_at = ((z, zb, zf, zo), (x, xb, xf, xo))

    def ag1(k):
        for h in range(2):
            own = one(k, x, z, h)
            for n in range(3):
                move(own, own, k, AG_P1 + 3 * h + n, near_to[h][n])

    def ag3(k):
        for h in range(2):
            for n, i in enumerate((1, 0, 2)):
                arrived(near(k, h, near_at[h][n + 1]), k, AG_P1 + 3 * h + n, near_to[h][i])
            own = line(k, h, far_at[h][0], c)
            move(own, own, k, AG_P2 + 3 * h, far_to[h][0])
            move(own, own, k, AG_P2 + 3 * h + 1, far_to[h][1])
            move(own, own, k, AG_SIB + 4 * h, to_sib)

    def ag4(k):
        for h in range(2):
            behind = line(k, h, far_at[h][1], c)
            arrived(behind, k, AG_P2 + 3 * h, far_to[h][1])
            move(behind, behind, k, AG_P2 + 3 * h + 2, far_to[h][0])
            move(behind, behind, k, AG_SIB + 4 * h + 1, to_sib)
        for h in range(2):
            ahead = line(k, h, far_at[h][2], c)
            arrived(ahead, k, AG_P2 + 3 * h + 1, far_to[h][0])
            move(ahead, ahead, k, AG_SIB + 4 * h + 2, to_sib)

    def ag5(k):
        for h in range(2):
            opposite = line(k, h, far_at[h][3], c)
            arrived(opposite, k, AG_P2 + 3 * h + 2, far_to[h][1])
            move(opposite, opposite, k, AG_SIB + 4 * h + 3, to_sib)

    def ag6(k):
        for h in range(2):
            at = far_at[h]
            for n, i in enumerate((0, 2, 1, 3)):
                arrived(line(k, h, at[i], 1 - c), k, AG_SIB + 4 * h + n, to_sib)

    def hidden(j):
        for copy in hidden_copies(j):
            copy.wait()
        part_sum = jnp.dot(wd_buf[j % 2], og_buf[j % 2], preferred_element_type=F32)
        if j == 0:
            hid[...] = part_sum
        else:
            hid[...] += part_sum
        if j + 2 < D // KB:
            for copy in hidden_copies(j + 2):
                copy.start()

    def gates(k, i):
        if k == 0 and i == 0:
            for n in (4, 0, 1):
                local[n].wait()
        at = i * rows
        wide = x_all[k, i].reshape(rows, tok).astype(F32)
        scale = gain[at:at + rows, :].astype(F32)
        scale = jnp.concatenate([scale] * (tok // 128), axis=1)
        y_buf[...] = (wide * scale).astype(BF16)
        part_squares = jnp.sum((wide * wide).reshape(rows // 8, 8, tok), axis=0)
        product = jnp.dot(w_in[:, at:at + rows], y_buf[...], preferred_element_type=F32)
        if i == 0:
            acc[...] = product
            squares[...] = part_squares
        else:
            acc[...] += product
            squares[...] += part_squares
        if i == SIDE - 1:
            activate(k)

    def activate(k):
        mean = jnp.sum(squares[...], axis=0, keepdims=True) / D
        inverse = lax.rsqrt(mean + 1e-06)
        inv_s[k] = jnp.broadcast_to(inverse, (8, tok))
        gate_out = acc[0:half] * inverse
        up_out = acc[half:2 * half] * inverse
        hidden_grad = hid[:, k * tok:(k + 1) * tok]
        sigma = jax.nn.sigmoid(gate_out)
        gate_grad = (hidden_grad * up_out * (sigma * (1.0 + gate_out * (1.0 - sigma)))).astype(BF16)
        up_grad = (hidden_grad * (gate_out * sigma)).astype(BF16)
        both[0:half] = gate_grad
        both[half:2 * half] = up_grad
        dots = jnp.sum(gate_grad.astype(F32) * gate_out + up_grad.astype(F32) * up_out, axis=0, keepdims=True)
        dp_[k] = jnp.broadcast_to(dots, (8, tok))
        move(dp_.at[k], dq.at[k], k, DOT_SIB, to_sib)

    def last(k, i):
        if k == 0 and i == 0:
            for n in (2, 3):
                local[n].wait()
        at = i * rows
        term = jnp.dot(w_out[at:at + rows, :], both[...], preferred_element_type=F32)
        part[k, i] = term.astype(BF16).reshape(SIDE, 2, 2, HALF, tok)
        move(part.at[k, i, :, 1 - c], sib_in.at[k, i], k, RS_SIB + i, to_sib)

    def add(*refs_):
        total = refs_[0].astype(F32)
        for other in refs_[1:]:
            total = total + other.astype(F32)
        return total

    def chip_line(k, h, at):
        return part.at[k, at, :, c, 0] if h == 0 else part.at[k, :, at, c, 1]

    def rs0(k):
        for i in range(SIDE):
            arrived(sib_in.at[k, i], k, RS_SIB + i, to_sib)
            part[k, i, :, c] = add(part[k, i, :, c], sib_in[k, i]).astype(BF16)
        for h in range(2):
            move(chip_line(k, h, far_at[h][3]), ra.at[k, h], k, RS_R1 + 3 * h, far_to[h][0])
        for h in range(2):
            move(chip_line(k, h, far_at[h][1]), rb.at[k, h], k, RS_R1 + 3 * h + 1, far_to[h][1])
        arrived(dq.at[k], k, DOT_SIB, to_sib)
        ds[k] = dp_[k] + dq[k]

    def rs0b(k):
        move(ds.at[k], dxf.at[k], k, DOT_X, to_xf)
        move(ds.at[k], dxb.at[k], k, DOT_X + 1, to_xb)
        move(ds.at[k], dxo.at[k], k, DOT_X + 2, to_xo)

    def rs1(k):
        for h in range(2):
            arrived(ra.at[k, h], k, RS_R1 + 3 * h, far_to[h][1])
            rst[k, h] = add(ra[k, h], chip_line(k, h, far_at[h][2])[...]).astype(BF16)
            move(rst.at[k, h], rc.at[k, h], k, RS_R1 + 3 * h + 2, far_to[h][0])

    def rs2(k):
        for h in range(2):
            arrived(rb.at[k, h], k, RS_R1 + 3 * h + 1, far_to[h][0])
            arrived(rc.at[k, h], k, RS_R1 + 3 * h + 2, far_to[h][1])
            rsum[k, h] = add(chip_line(k, h, far_at[h][0])[...], rb[k, h], rc[k, h]).astype(BF16)
            for n, i in enumerate((2, 1, 3)):
                move(rsum.at[k, h, near_at[h][i]], (qa, qb, qc)[n].at[k, h], k, RS_R2 + 3 * h + n, near_to[h][n])
        arrived(dxf.at[k], k, DOT_X, to_xb)
        arrived(dxb.at[k], k, DOT_X + 1, to_xf)
        arrived(dxo.at[k], k, DOT_X + 2, to_xo)
        dr[k] = ds[k] + dxf[k] + dxb[k] + dxo[k]
        move(dr.at[k], dzf.at[k], k, DOT_Z, to_zf)
        move(dr.at[k], dzb.at[k], k, DOT_Z + 1, to_zb)
        move(dr.at[k], dzo.at[k], k, DOT_Z + 2, to_zo)

    def rs4(k):
        arrived(dzf.at[k], k, DOT_Z, to_zb)
        arrived(dzb.at[k], k, DOT_Z + 1, to_zf)
        arrived(dzo.at[k], k, DOT_Z + 2, to_zo)
        dots = (dr[k] + dzf[k] + dzb[k] + dzo[k])[0:1]
        inverse = inv_s[k][0:1]
        pull = dots * inverse * inverse / D
        for h in range(2):
            for n, i in enumerate((1, 0, 2)):
                arrived((qa, qb, qc)[n].at[k, h], k, RS_R2 + 3 * h + n, near_to[h][i])
            norm_grad = add(rsum[k, h, near_at[h][0]], qa[k, h], qb[k, h], qc[k, h])
            span = slice(h * HALF, (h + 1) * HALF)
            cols = slice(k * tok, (k + 1) * tok)
            full = og_own_ref[span, cols].astype(F32) + gain_own_ref[span, 0:1].astype(F32) * inverse * norm_grad
            full = full - res_ref[span, cols].astype(F32) * pull
            out_ref[span, cols] = full.astype(BF16)

    for k in range(CHUNKS):
        ag1(k)
    hidden(0)
    local[0].start()
    local[1].start()
    hidden(1)
    ag3(0)
    ag3(1)
    hidden(2)
    hidden(3)
    hidden(4)
    ag4(0)
    ag3(2)
    hidden(5)
    local[2].start()
    local[3].start()
    hidden(6)
    ag5(0)
    ag4(1)
    hidden(7)
    ag6(0)
    gates(0, 0)
    ag5(1)
    gates(0, 1)
    gates(0, 2)
    ag4(2)
    gates(0, 3)
    last(0, 0)
    last(0, 1)
    last(0, 2)
    ag5(2)
    last(0, 3)
    ag6(1)
    gates(1, 0)
    rs0(0)
    rs0b(0)
    gates(1, 1)
    gates(1, 2)
    gates(1, 3)
    last(1, 0)
    last(1, 1)
    rs1(0)
    last(1, 2)
    last(1, 3)
    ag6(2)
    gates(2, 0)
    rs0(1)
    rs0b(1)
    gates(2, 1)
    rs2(0)
    gates(2, 2)
    gates(2, 3)
    last(2, 0)
    last(2, 1)
    rs1(1)
    last(2, 2)
    last(2, 3)
    rs0(2)
    rs0b(2)
    rs2(1)
    rs4(0)
    rs1(2)
    rs4(1)
    rs2(2)
    rs4(2)
    for copy in sent:
        copy.wait_send()


def core(residual, out_grad_t, gain_own, og_ext, w_down, w_gate, w_up, w_gate_t, w_up_t):
    width = residual.shape[1]
    tok = width // CHUNKS
    hid = w_gate.shape[1]
    vm = pl.BlockSpec(memory_space=pltpu.VMEM)
    hbm = pl.BlockSpec(memory_space=pl.ANY)

    def bf(*shape):
        return pltpu.VMEM(shape, BF16)

    def fl(*shape):
        return pltpu.VMEM(shape, F32)

    rows = SIDE * 2 * 2 * HALF
    return pl.pallas_call(
        core_kernel,
        out_shape=jax.ShapeDtypeStruct(residual.shape, BF16),
        in_specs=[vm] * 3 + [hbm] * 6,
        out_specs=vm,
        scratch_shapes=[
            bf(CHUNKS, SIDE, SIDE, 2, 2, HALF, tok),
            bf(D, 2 * hid), bf(2 * hid, D),
            bf(D, 128),
            bf(2, KB, width), bf(2, hid, KB),
            fl(hid, width),
            bf(rows, tok), fl(2 * hid, tok), fl(8, tok), bf(2 * hid, tok), fl(CHUNKS, 8, tok),
            bf(CHUNKS, SIDE, SIDE, 2, 2, HALF, tok), bf(CHUNKS, SIDE, SIDE, 2, HALF, tok),
        ]
        + [bf(CHUNKS, 2, SIDE, HALF, tok)] * 5
        + [bf(CHUNKS, 2, HALF, tok)] * 3
        + [fl(CHUNKS, 8, tok)] * 10
        + [
            pltpu.SemaphoreType.DMA((CHUNKS, SLOTS)),
            pltpu.SemaphoreType.DMA((CHUNKS, SLOTS)),
            pltpu.SemaphoreType.DMA((5,)),
            pltpu.SemaphoreType.DMA((2, 2)),
        ],
        compiler_params=pltpu.CompilerParams(
            collective_id=0, has_side_effects=True, vmem_limit_bytes=60 * 1024 * 1024
        ),
        cost_estimate=pl.CostEstimate(flops=10 * D * hid * width, bytes_accessed=40_000_000, transcendentals=0),
        name="core",
    )(residual, out_grad_t, gain_own, og_ext, w_down, w_gate, w_up, w_gate_t, w_up_t)


MESH = pl.DeviceIdType.MESH
SLOT = 32
SPANS = ((0, 512), (512, 384))


def nt(a, b):
    return lax.dot_general(a, b, (((1,), (1,)), ((), ())), preferred_element_type=F32)


def fetch_kernel(
    tok_ref, og_ref, ten_ref, halves_ref, table_hbm, wg_hbm, wu_hbm,
    res_ref, og_out, wanted_ref, place_ref, wgt_hbm, wut_hbm,
    tbuf, earlier, rows_s, rows_r, turned, landed, acc, w_buf, wt_buf, table_ref,
    tsend, trecv, ysend, yrecv, psend, precv, gsend, grecv, lsem,
):
    d = lax.axis_index("dp")
    t = lax.axis_index("tensor")
    me = d * 32 + t
    x = t // 8
    z = lax.rem(t // 2, 4)
    c = lax.rem(t, 2)
    step = 1 - 2 * c
    xf, xb, xo = lax.rem(x + step + 4, 4), lax.rem(x - step + 4, 4), lax.rem(x + 2, 4)
    zf, zb, zo = lax.rem(z + step + 4, 4), lax.rem(z - step + 4, 4), lax.rem(z + 2, 4)

    def dev(xx, zz, cc):
        return {"dp": d, "tensor": (xx * 4 + zz) * 2 + cc}

    to_xf, to_xb = dev(xf, z, c), dev(xb, z, c)
    to_zf, to_zb = dev(x, zf, c), dev(x, zb, c)
    to_xo, to_zo = dev(xo, z, c), dev(x, zo, c)
    to_sib = dev(x, z, 1 - c)
    width = tok_ref.shape[1]
    feat = tok_ref.shape[0]
    parts = D // feat

    own_copies = [
        pltpu.make_async_copy(og_ref.at[pl.ds(h * HALF, HALF)], og_out.at[x, z, c, h], lsem.at[h]) for h in range(2)
    ]
    for copy in own_copies:
        copy.start()
    w_in = [pltpu.make_async_copy(src, w_buf.at[n], lsem.at[2 + n]) for n, src in enumerate((wg_hbm, wu_hbm))]
    w_out = [pltpu.make_async_copy(wt_buf.at[n], dst, lsem.at[4 + n]) for n, dst in enumerate((wgt_hbm, wut_hbm))]
    table_in = pltpu.make_async_copy(table_hbm, table_ref, lsem.at[6])
    table_in.start()
    for copy in w_in:
        copy.start()
    barrier = pltpu.get_barrier_semaphore()

    def greet(o, carry):
        pl.semaphore_signal(
            barrier, inc=1, device_id={"dp": d, "tensor": lax.rem(t + o, parts)}, device_id_type=MESH
        )
        return carry

    lax.fori_loop(1, parts, greet, 0)
    for o in (1, 2, 3):
        pl.semaphore_signal(barrier, inc=1, device_id={"dp": lax.rem(d + o, 4), "tensor": t}, device_id_type=MESH)
    pl.semaphore_wait(barrier, parts - 1 + 3)

    sent = []

    def send(src, dst, ssem, rsem, where):
        copy = pltpu.make_async_remote_copy(
            src_ref=src, dst_ref=dst, send_sem=ssem, recv_sem=rsem, device_id=where, device_id_type=MESH
        )
        copy.start()
        sent.append(copy)

    def got(dst, ssem, rsem, where):
        pltpu.make_async_remote_copy(
            src_ref=dst, dst_ref=dst, send_sem=ssem, recv_sem=rsem, device_id=where, device_id_type=MESH
        ).wait_recv()

    for o in (1, 3, 2):
        there = lax.rem(d + o, 4)
        send(ten_ref, tbuf.at[d], tsend.at[there], trecv.at[d], {"dp": there, "tensor": t})

    near_to = ((to_zf, to_zb, to_zo), (to_xf, to_xb, to_xo))
    far_to = ((to_xf, to_xb), (to_zf, to_zb))
    near_at = ((z, zb, zf, zo), (x, xb, xf, xo))
    far_at = ((x, xb, xf, xo), (z, zb, zf, zo))

    def lanes(k):
        return pl.ds(SPANS[k][0], SPANS[k][1])

    def near(k, h, at):
        return og_out.at[x, at, c, 0, :, lanes(k)] if h == 0 else og_out.at[at, z, c, 1, :, lanes(k)]

    def line(k, h, at, cc):
        return og_out.at[at, :, cc, 0, :, lanes(k)] if h == 0 else og_out.at[:, at, cc, 1, :, lanes(k)]

    def move(src, dst, k, slot, where):
        send(src, dst, gsend.at[k, slot], grecv.at[k, slot], where)

    def arrived(dst, k, slot, where):
        got(dst, gsend.at[k, slot], grecv.at[k, slot], where)

    def ag1(k):
        for h in range(2):
            own = near(k, h, near_at[h][0])
            src = og_ref.at[pl.ds(h * HALF, HALF), lanes(k)]
            for n in range(3):
                move(src, own, k, AG_P1 + 3 * h + n, near_to[h][n])

    def ag3(k):
        for h in range(2):
            for n, i in enumerate((1, 0, 2)):
                arrived(near(k, h, near_at[h][n + 1]), k, AG_P1 + 3 * h + n, near_to[h][i])
            own = line(k, h, far_at[h][0], c)
            move(own, own, k, AG_P2 + 3 * h, far_to[h][0])
            move(own, own, k, AG_P2 + 3 * h + 1, far_to[h][1])
            move(own, own, k, AG_SIB + 4 * h, to_sib)

    def ag4(k):
        for h in range(2):
            behind = line(k, h, far_at[h][1], c)
            arrived(behind, k, AG_P2 + 3 * h, far_to[h][1])
            move(behind, behind, k, AG_P2 + 3 * h + 2, far_to[h][0])
            move(behind, behind, k, AG_SIB + 4 * h + 1, to_sib)
        for h in range(2):
            ahead = line(k, h, far_at[h][2], c)
            arrived(ahead, k, AG_P2 + 3 * h + 1, far_to[h][0])
            move(ahead, ahead, k, AG_SIB + 4 * h + 2, to_sib)

    def ag5(k):
        for h in range(2):
            opposite = line(k, h, far_at[h][3], c)
            arrived(opposite, k, AG_P2 + 3 * h + 2, far_to[h][1])
            move(opposite, opposite, k, AG_SIB + 4 * h + 3, to_sib)

    def ag6(k):
        for h in range(2):
            for n, i in enumerate((0, 2, 1, 3)):
                arrived(line(k, h, far_at[h][i], 1 - c), k, AG_SIB + 4 * h + n, to_sib)

    ag1(0)
    ag1(1)

    lines = halves_ref.shape[1]
    earlier[...] = (
        lax.broadcasted_iota(jnp.int32, (width, width), 0) < lax.broadcasted_iota(jnp.int32, (width, width), 1)
    ).astype(F32).astype(BF16)

    def hot(index, size):
        return (lax.broadcasted_iota(jnp.int32, (size, width), 0) == index).astype(F32)

    def look_up(tenant):
        picked = jnp.dot(halves_ref[...], hot(tenant // 128, lines).astype(BF16), preferred_element_type=F32)
        lane = hot(lax.rem(tenant, 128), 128)
        owner = jnp.sum(lane * picked[:128], axis=0, keepdims=True).astype(jnp.int32)
        row = jnp.sum(lane * picked[128:], axis=0, keepdims=True).astype(jnp.int32)
        return owner, row

    def ranks(matches):
        before = jnp.dot(matches.astype(BF16), earlier[...], preferred_element_type=F32)
        return jnp.sum(matches * before, axis=0, keepdims=True).astype(jnp.int32)

    owner, row = look_up(ten_ref[0:1])
    rank = ranks(hot(owner, 128))
    place = lax.rem(owner, 32) * 128 + owner // 32 * SLOT + rank
    place_ref[...] = jnp.broadcast_to(place, place_ref.shape)

    tbuf[d] = ten_ref[...]
    for o in (1, 3, 2):
        there = lax.rem(d + o, 4)
        got(tbuf.at[there], tsend.at[there], trecv.at[there], {"dp": there, "tensor": t})
    for g in range(4):
        owner, row = look_up(tbuf[g, 0:1])
        mine = (owner == me).astype(F32)
        mine8 = jnp.broadcast_to(mine, (8, width))
        before = jnp.dot(mine8.astype(BF16), earlier[...], preferred_element_type=F32)[0:1]
        slot = jnp.where(mine > 0, before.astype(jnp.int32), -1)
        wanted = nt(hot(slot, SLOT).astype(BF16), hot(row, table_ref.shape[0]).astype(BF16)).astype(BF16)
        wanted_ref[g * SLOT:(g + 1) * SLOT] = wanted

    quarter = D // 4

    def y_copy(q, there, at):
        return pltpu.make_async_remote_copy(
            src_ref=rows_s.at[q, there], dst_ref=rows_r.at[q, at], send_sem=ysend.at[q, there], recv_sem=yrecv.at[q, at],
            device_id={"dp": there, "tensor": t}, device_id_type=MESH,
        )

    others = tuple(lax.rem(d + o, 4) for o in (1, 3, 2))
    order = (x, lax.rem(x + 1, 4), lax.rem(x + 3, 4), xo)

    def pick(q):
        cols = pl.ds(pl.multiple_of(q * quarter, quarter), quarter)
        picked = jnp.dot(wanted_ref[...], table_ref[:, cols], preferred_element_type=F32)
        rows_s[q] = picked.astype(BF16).reshape(4, SLOT, quarter)
        for there in others:
            y_copy(q, there, d).start()
        rows_r[q, d] = rows_s[q, d]

    table_in.wait()
    for q in order:
        pick(q)
    for copy in own_copies:
        copy.wait()
    ag3(0)
    ag3(1)

    def turn_weight(n):
        w_in[n].wait()
        wide = 640

        def body(i, carry):
            at = pl.multiple_of(i * wide, wide)
            wt_buf[n, :, pl.ds(at, wide)] = w_buf[n, pl.ds(at, wide), :].T
            return carry

        lax.fori_loop(0, D // wide, body, 0)
        w_out[n].start()

    def plane_copy(there):
        return pltpu.make_async_remote_copy(
            src_ref=turned.at[there], dst_ref=landed.at[t], send_sem=psend.at[there], recv_sem=precv.at[t],
            device_id={"dp": d, "tensor": there}, device_id_type=MESH,
        )

    row = parts // 4

    def pass_on(n):
        q = order[n]
        for there in others:
            pltpu.make_async_remote_copy(
                src_ref=rows_r.at[q, there], dst_ref=rows_r.at[q, there],
                send_sem=ysend.at[q, there], recv_sem=yrecv.at[q, there],
                device_id={"dp": there, "tensor": t}, device_id_type=MESH,
            ).wait_recv()
        turned[pl.ds(q * row, row)] = rows_r[q].reshape(4 * SLOT, quarter).T.reshape(row, feat, 4 * SLOT)

        def scatter(i, carry):
            plane_copy(q * row + lax.rem(lax.rem(t, row) + i, row)).start()
            return carry

        lax.fori_loop(1 if n == 0 else 0, row, scatter, 0)
        if n == 0:
            landed[t] = turned[t]

    turn_weight(0)
    pass_on(0)
    ag4(0)
    pass_on(1)
    pass_on(2)
    pass_on(3)
    acc[...] = tok_ref[...].astype(F32)
    turn_weight(1)
    ag4(1)
    ag5(0)

    def arrive(src):
        @pl.when(src != t)
        def _():
            pltpu.make_async_remote_copy(
                src_ref=landed.at[src], dst_ref=landed.at[src], send_sem=psend.at[src], recv_sem=precv.at[src],
                device_id={"dp": d, "tensor": src}, device_id_type=MESH,
            ).wait_recv()

    def gather(q):
        def body(i, carry):
            pair = q * (row // 2) + i
            arrive(2 * pair)
            arrive(2 * pair + 1)
            sel = (lax.broadcasted_iota(jnp.int32, (256, width), 0) + pair * 256 == place).astype(F32).astype(BF16)
            both = jnp.concatenate([landed[2 * pair], landed[2 * pair + 1]], axis=1)
            acc[...] += jnp.dot(both, sel, preferred_element_type=F32)
            return carry

        lax.fori_loop(0, row // 2, body, 0)

    gather(x)
    ag5(1)
    gather(order[2])
    gather(order[1])
    ag6(0)
    gather(xo)
    res_ref[...] = acc[...].astype(BF16)
    ag6(1)

    def drain(o, carry):
        plane_copy(lax.rem(t + o, parts)).wait_send()
        return carry

    lax.fori_loop(1, parts, drain, 0)
    for q in range(4):
        for there in others:
            y_copy(q, there, d).wait_send()
    for copy in sent:
        copy.wait_send()
    for copy in w_out:
        copy.wait()


def fetch(tokens_t, og_ext, tenant8, halves, table, w_gate, w_up):
    feat, width = tokens_t.shape
    parts = D // feat
    vm = pl.BlockSpec(memory_space=pltpu.VMEM)
    hbm = pl.BlockSpec(memory_space=pl.ANY)
    dma = pltpu.SemaphoreType.DMA
    return pl.pallas_call(
        fetch_kernel,
        out_shape=(
            jax.ShapeDtypeStruct((feat, width), BF16),
            jax.ShapeDtypeStruct((SIDE, SIDE, 2, 2, HALF, og_ext.shape[1]), BF16),
            jax.ShapeDtypeStruct((4 * SLOT, table.shape[0]), BF16),
            jax.ShapeDtypeStruct((8, width), jnp.int32),
            jax.ShapeDtypeStruct(w_gate.shape[::-1], BF16),
            jax.ShapeDtypeStruct(w_up.shape[::-1], BF16),
        ),
        in_specs=[vm] * 4 + [hbm] * 3,
        out_specs=(vm, hbm, vm, vm, hbm, hbm),
        scratch_shapes=[
            pltpu.VMEM((4, 8, width), jnp.int32),
            pltpu.VMEM((width, width), BF16),
            pltpu.VMEM((4, 4, SLOT, D // 4), BF16),
            pltpu.VMEM((4, 4, SLOT, D // 4), BF16),
            pltpu.VMEM((parts, feat, 4 * SLOT), BF16),
            pltpu.VMEM((parts, feat, 4 * SLOT), BF16),
            pltpu.VMEM((feat, width), F32),
            pltpu.VMEM((2,) + w_gate.shape, BF16),
            pltpu.VMEM((2,) + w_gate.shape[::-1], BF16),
            pltpu.VMEM(table.shape, BF16),
            dma((4,)), dma((4,)), dma((4, 4)), dma((4, 4)), dma((parts,)), dma((parts,)),
            dma((len(SPANS), RS_SIB)), dma((len(SPANS), RS_SIB)), dma((7,)),
        ],
        compiler_params=pltpu.CompilerParams(
            collective_id=1, has_side_effects=True, vmem_limit_bytes=48 * 1024 * 1024
        ),
        cost_estimate=pl.CostEstimate(flops=4_000_000_000, bytes_accessed=20_000_000, transcendentals=0),
        name="fetch",
    )(tokens_t, og_ext, tenant8, halves, table, w_gate, w_up)


def give_kernel(full_ref, place_ref, rows_r, leaving, landed, rows_s, psend, precv, ysend, yrecv):
    d = lax.axis_index("dp")
    t = lax.axis_index("tensor")
    feat, width = full_ref.shape
    parts = D // feat
    barrier = pltpu.get_barrier_semaphore()

    def greet(o, carry):
        pl.semaphore_signal(
            barrier, inc=1, device_id={"dp": d, "tensor": lax.rem(t + o, parts)}, device_id_type=MESH
        )
        return carry

    lax.fori_loop(1, parts, greet, 0)
    for o in (1, 2, 3):
        pl.semaphore_signal(barrier, inc=1, device_id={"dp": lax.rem(d + o, 4), "tensor": t}, device_id_type=MESH)

    place = place_ref[0:1]
    pl.semaphore_wait(barrier, parts - 1 + 3)

    def plane_copy(there, at):
        return pltpu.make_async_remote_copy(
            src_ref=leaving.at[there], dst_ref=landed.at[at], send_sem=psend.at[there], recv_sem=precv.at[at],
            device_id={"dp": d, "tensor": there}, device_id_type=MESH,
        )

    def pack(pair):
        sel = (lax.broadcasted_iota(jnp.int32, (256, width), 0) + pair * 256 == place).astype(F32).astype(BF16)
        packed = nt(full_ref[...], sel).astype(BF16)
        for half in range(2):
            there = 2 * pair + half
            leaving[there] = packed[:, 128 * half:128 * half + 128]

            @pl.when(there != t)
            def _():
                plane_copy(there, t).start()

    quad = parts // 8
    x = t // 8

    def own_row(i, carry):
        pack(x * quad + lax.rem(lax.rem(t // 2, quad) + i, quad))
        return carry

    def side_rows(i, carry):
        at = lax.rem(lax.rem(t // 2, quad) + i, quad)
        pack(lax.rem(x + 1, 4) * quad + at)
        pack(lax.rem(x + 3, 4) * quad + at)
        return carry

    def far_row(i, carry):
        pack(lax.rem(x + 2, 4) * quad + lax.rem(lax.rem(t // 2, quad) + i, quad))
        return carry

    lax.fori_loop(0, quad, own_row, 0)
    landed[t] = leaving[t]
    lax.fori_loop(0, quad, side_rows, 0)
    lax.fori_loop(0, quad, far_row, 0)

    group = 8

    def y_copy(q, there):
        return pltpu.make_async_remote_copy(
            src_ref=rows_s.at[q, there], dst_ref=rows_r.at[q, d], send_sem=ysend.at[q, there], recv_sem=yrecv.at[q, d],
            device_id={"dp": there, "tensor": t}, device_id_type=MESH,
        )

    def arrive(src):
        @pl.when(src != t)
        def _():
            pltpu.make_async_remote_copy(
                src_ref=landed.at[src], dst_ref=landed.at[src], send_sem=psend.at[src], recv_sem=precv.at[src],
                device_id={"dp": d, "tensor": src}, device_id_type=MESH,
            ).wait_recv()

    for q in (x, lax.rem(x + 3, 4), lax.rem(x + 1, 4), lax.rem(x + 2, 4)):

        def take(i, inner):
            arrive(q * group + i)
            return inner

        lax.fori_loop(0, group, take, 0)
        block = landed[pl.ds(q * group, group)].reshape(group * feat, 4 * SLOT)
        rows_s[q] = block.T.reshape(4, SLOT, group * feat)
        for o in (1, 3, 2):
            y_copy(q, lax.rem(d + o, 4)).start()
        rows_r[q, d] = rows_s[q, d]

    def finish(q, carry):
        for o in (1, 3, 2):
            there = lax.rem(d + o, 4)
            y_copy(q, there).wait_send()
            pltpu.make_async_remote_copy(
                src_ref=rows_r.at[q, there], dst_ref=rows_r.at[q, there],
                send_sem=ysend.at[q, there], recv_sem=yrecv.at[q, there],
                device_id={"dp": there, "tensor": t}, device_id_type=MESH,
            ).wait_recv()
        return carry

    lax.fori_loop(0, 4, finish, 0)

    def drain(o, carry):
        plane_copy(lax.rem(t + o, parts), t).wait_send()
        return carry

    lax.fori_loop(1, parts, drain, 0)


def give(full_grad, place):
    feat, width = full_grad.shape
    parts = D // feat
    vm = pl.BlockSpec(memory_space=pltpu.VMEM)
    dma = pltpu.SemaphoreType.DMA
    return pl.pallas_call(
        give_kernel,
        out_shape=jax.ShapeDtypeStruct((4, 4, SLOT, D // 4), BF16),
        in_specs=[vm] * 2,
        out_specs=vm,
        scratch_shapes=[
            pltpu.VMEM((parts, feat, 4 * SLOT), BF16),
            pltpu.VMEM((parts, feat, 4 * SLOT), BF16),
            pltpu.VMEM((4, 4, SLOT, D // 4), BF16),
            dma((parts,)), dma((parts,)), dma((4, 4)), dma((4, 4)),
        ],
        compiler_params=pltpu.CompilerParams(
            collective_id=2, has_side_effects=True, vmem_limit_bytes=48 * 1024 * 1024
        ),
        cost_estimate=pl.CostEstimate(flops=2_000_000_000, bytes_accessed=3_000_000, transcendentals=0),
        name="give",
    )(full_grad, place)


def per_device(tokens_in, out_grad, tenant, slot_of, steer_table, norm_gain, w_gate, w_up, w_down):
    feat_local = tokens_in.shape[1]
    token_count = tenant.shape[0]
    out_grad_t = out_grad.T
    gain_own = jnp.broadcast_to(norm_gain[:, None], (feat_local, 128))
    lines = slot_of.reshape(-1, 128).T
    halves = jnp.concatenate([lines // 256, lines % 256], axis=0).astype(BF16)
    tenant8 = jnp.broadcast_to(tenant[None, :], (8, token_count))
    residual, og_ext, wanted, place, w_gate_t, w_up_t = fetch(
        tokens_in.T, jnp.concatenate([out_grad_t, gain_own], axis=1), tenant8, halves, steer_table, w_gate, w_up
    )
    og_ext = og_ext.reshape(D, token_count + 128)
    full_grad = core(residual, out_grad_t, gain_own, og_ext, w_down, w_gate, w_up, w_gate_t, w_up_t)
    rows = give(full_grad, place)
    rows = rows.transpose(1, 2, 0, 3).reshape(4 * SLOT, D)
    table_grad = lax.dot_general(wanted, rows, (((0,), (0,)), ((), ())), preferred_element_type=F32)
    return (full_grad.T, table_grad)


def solution(mesh):
    placed = (
        P("dp", "tensor"),
        P("dp", "tensor"),
        P("dp"),
        P(),
        P(("dp", "tensor"), None),
        P("tensor"),
        P(None, "tensor"),
        P(None, "tensor"),
        P("tensor", None),
    )
    return jax.shard_map(
        per_device,
        mesh=mesh,
        in_specs=placed,
        out_specs=(P("dp", "tensor"), P(("dp", "tensor"), None)),
        check_vma=False,
    )
```

```python
import functools

import jax
import jax.numpy as jnp
from jax import lax
from jax.experimental import pallas as pl
from jax.experimental.pallas import tpu as pltpu
from jax.sharding import PartitionSpec as P

D = 5120
F32 = jnp.float32
BF16 = jnp.bfloat16


CHUNKS = 3
SIDE = 4
HALF = 80
KB = 640
AG_P1 = 0
AG_P2 = 6
AG_SIB = 12
RS_SIB = 20
RS_R1 = 24
RS_R2 = 30
DOT_SIB = 36
DOT_X = 37
DOT_Z = 40
SLOTS = 43


def core_kernel(
    res_ref, og_own_ref, gain_own_ref, og_hbm, wd_hbm, wg_hbm, wu_hbm, wgt_hbm, wut_hbm,
    out_ref,
    x_all, w_out, w_in, gain, og_buf, wd_buf, hid, y_buf, acc, squares, both, inv_s,
    part, sib_in, ra, rb, rc, rst, rsum, qa, qb, qc,
    dp_, ds, dq, dxf, dxb, dxo, dr, dzf, dzb, dzo,
    ssem, rsem, lsem, hsem,
):
    ten = lax.axis_index("tensor")
    x = ten // 8
    z = lax.rem(ten // 2, 4)
    c = lax.rem(ten, 2)
    step = 1 - 2 * c
    xf, xb, xo = lax.rem(x + step + 4, 4), lax.rem(x - step + 4, 4), lax.rem(x + 2, 4)
    zf, zb, zo = lax.rem(z + step + 4, 4), lax.rem(z - step + 4, 4), lax.rem(z + 2, 4)

    def dev(xx, zz, cc):
        return {"tensor": (xx * 4 + zz) * 2 + cc}

    to_xf, to_xb = dev(xf, z, c), dev(xb, z, c)
    to_zf, to_zb = dev(x, zf, c), dev(x, zb, c)
    to_xo, to_zo = dev(xo, z, c), dev(x, zo, c)
    to_sib = dev(x, z, 1 - c)
    width = res_ref.shape[1]
    tok = width // CHUNKS
    rows = SIDE * 2 * 2 * HALF

    half = wg_hbm.shape[1]
    local = [
        pltpu.make_async_copy(wgt_hbm, w_in.at[pl.ds(0, half)], lsem.at[0]),
        pltpu.make_async_copy(wut_hbm, w_in.at[pl.ds(half, half)], lsem.at[1]),
        pltpu.make_async_copy(wg_hbm, w_out.at[:, pl.ds(0, half)], lsem.at[2]),
        pltpu.make_async_copy(wu_hbm, w_out.at[:, pl.ds(half, half)], lsem.at[3]),
        pltpu.make_async_copy(og_hbm.at[:, pl.ds(width, 128)], gain, lsem.at[4]),
    ]

    def hidden_copies(j):
        return (
            pltpu.make_async_copy(og_hbm.at[pl.ds(j * KB, KB), pl.ds(0, width)], og_buf.at[j % 2], hsem.at[0, j % 2]),
            pltpu.make_async_copy(wd_hbm.at[:, pl.ds(j * KB, KB)], wd_buf.at[j % 2], hsem.at[1, j % 2]),
        )

    for copy in hidden_copies(0) + hidden_copies(1):
        copy.start()
    local[4].start()

    for k in range(CHUNKS):
        for h in range(2):
            x_all[k, x, z, c, h] = res_ref[h * HALF:(h + 1) * HALF, k * tok:(k + 1) * tok]

    barrier = pltpu.get_barrier_semaphore()
    for where in (to_xf, to_xb, to_xo, to_zf, to_zb, to_zo, to_sib):
        pl.semaphore_signal(barrier, inc=1, device_id=where, device_id_type=pl.DeviceIdType.MESH)
    pl.semaphore_wait(barrier, 7)

    sent = []

    def move(src, dst, k, slot, where):
        copy = pltpu.make_async_remote_copy(
            src_ref=src, dst_ref=dst, send_sem=ssem.at[k, slot], recv_sem=rsem.at[k, slot],
            device_id=where, device_id_type=pl.DeviceIdType.MESH,
        )
        copy.start()
        sent.append(copy)

    def arrived(dst, k, slot, where):
        pltpu.make_async_remote_copy(
            src_ref=dst, dst_ref=dst, send_sem=ssem.at[k, slot], recv_sem=rsem.at[k, slot],
            device_id=where, device_id_type=pl.DeviceIdType.MESH,
        ).wait_recv()

    def one(k, xx, zz, h):
        return x_all.at[k, xx, zz, c, h]

    def line(k, h, at, cc):
        return x_all.at[k, at, :, cc, 0] if h == 0 else x_all.at[k, :, at, cc, 1]

    near_to = ((to_zf, to_zb, to_zo), (to_xf, to_xb, to_xo))
    far_to = ((to_xf, to_xb), (to_zf, to_zb))
    far_at = ((x, xb, xf, xo), (z, zb, zf, zo))

    def near(k, h, at):
        return one(k, x, at, 0) if h == 0 else one(k, at, z, 1)

    near_at = ((z, zb, zf, zo), (x, xb, xf, xo))

    def ag1(k):
        for h in range(2):
            own = one(k, x, z, h)
            for n in range(3):
                move(own, own, k, AG_P1 + 3 * h + n, near_to[h][n])

    def ag3(k):
        for h in range(2):
            for n, i in enumerate((1, 0, 2)):
                arrived(near(k, h, near_at[h][n + 1]), k, AG_P1 + 3 * h + n, near_to[h][i])
            own = line(k, h, far_at[h][0], c)
            move(own, own, k, AG_P2 + 3 * h, far_to[h][0])
            move(own, own, k, AG_P2 + 3 * h + 1, far_to[h][1])
            move(own, own, k, AG_SIB + 4 * h, to_sib)

    def ag4(k):
        for h in range(2):
            behind = line(k, h, far_at[h][1], c)
            arrived(behind, k, AG_P2 + 3 * h, far_to[h][1])
            move(behind, behind, k, AG_P2 + 3 * h + 2, far_to[h][0])
            move(behind, behind, k, AG_SIB + 4 * h + 1, to_sib)
        for h in range(2):
            ahead = line(k, h, far_at[h][2], c)
            arrived(ahead, k, AG_P2 + 3 * h + 1, far_to[h][0])
            move(ahead, ahead, k, AG_SIB + 4 * h + 2, to_sib)

    def ag5(k):
        for h in range(2):
            opposite = line(k, h, far_at[h][3], c)
            arrived(opposite, k, AG_P2 + 3 * h + 2, far_to[h][1])
            move(opposite, opposite, k, AG_SIB + 4 * h + 3, to_sib)

    def ag6(k):
        for h in range(2):
            at = far_at[h]
            for n, i in enumerate((0, 2, 1, 3)):
                arrived(line(k, h, at[i], 1 - c), k, AG_SIB + 4 * h + n, to_sib)

    def hidden(j):
        for copy in hidden_copies(j):
            copy.wait()
        part_sum = jnp.dot(wd_buf[j % 2], og_buf[j % 2], preferred_element_type=F32)
        if j == 0:
            hid[...] = part_sum
        else:
            hid[...] += part_sum
        if j + 2 < D // KB:
            for copy in hidden_copies(j + 2):
                copy.start()

    def gates(k, i):
        if k == 0 and i == 0:
            for n in (4, 0, 1):
                local[n].wait()
        at = i * rows
        wide = x_all[k, i].reshape(rows, tok).astype(F32)
        scale = gain[at:at + rows, :].astype(F32)
        scale = jnp.concatenate([scale] * (tok // 128), axis=1)
        y_buf[...] = (wide * scale).astype(BF16)
        part_squares = jnp.sum((wide * wide).reshape(rows // 8, 8, tok), axis=0)
        product = jnp.dot(w_in[:, at:at + rows], y_buf[...], preferred_element_type=F32)
        if i == 0:
            acc[...] = product
            squares[...] = part_squares
        else:
            acc[...] += product
            squares[...] += part_squares
        if i == SIDE - 1:
            activate(k)

    def activate(k):
        mean = jnp.sum(squares[...], axis=0, keepdims=True) / D
        inverse = lax.rsqrt(mean + 1e-06)
        inv_s[k] = jnp.broadcast_to(inverse, (8, tok))
        gate_out = acc[0:half] * inverse
        up_out = acc[half:2 * half] * inverse
        hidden_grad = hid[:, k * tok:(k + 1) * tok]
        sigma = jax.nn.sigmoid(gate_out)
        gate_grad = (hidden_grad * up_out * (sigma * (1.0 + gate_out * (1.0 - sigma)))).astype(BF16)
        up_grad = (hidden_grad * (gate_out * sigma)).astype(BF16)
        both[0:half] = gate_grad
        both[half:2 * half] = up_grad
        dots = jnp.sum(gate_grad.astype(F32) * gate_out + up_grad.astype(F32) * up_out, axis=0, keepdims=True)
        dp_[k] = jnp.broadcast_to(dots, (8, tok))
        move(dp_.at[k], dq.at[k], k, DOT_SIB, to_sib)

    def last(k, i):
        if k == 0 and i == 0:
            for n in (2, 3):
                local[n].wait()
        at = i * rows
        term = jnp.dot(w_out[at:at + rows, :], both[...], preferred_element_type=F32)
        part[k, i] = term.astype(BF16).reshape(SIDE, 2, 2, HALF, tok)
        move(part.at[k, i, :, 1 - c], sib_in.at[k, i], k, RS_SIB + i, to_sib)

    def add(*refs_):
        total = refs_[0].astype(F32)
        for other in refs_[1:]:
            total = total + other.astype(F32)
        return total

    def chip_line(k, h, at):
        return part.at[k, at, :, c, 0] if h == 0 else part.at[k, :, at, c, 1]

    def rs0(k):
        for i in range(SIDE):
            arrived(sib_in.at[k, i], k, RS_SIB + i, to_sib)
            part[k, i, :, c] = add(part[k, i, :, c], sib_in[k, i]).astype(BF16)
        for h in range(2):
            move(chip_line(k, h, far_at[h][3]), ra.at[k, h], k, RS_R1 + 3 * h, far_to[h][0])
        for h in range(2):
            move(chip_line(k, h, far_at[h][1]), rb.at[k, h], k, RS_R1 + 3 * h + 1, far_to[h][1])
        arrived(dq.at[k], k, DOT_SIB, to_sib)
        ds[k] = dp_[k] + dq[k]

    def rs0b(k):
        move(ds.at[k], dxf.at[k], k, DOT_X, to_xf)
        move(ds.at[k], dxb.at[k], k, DOT_X + 1, to_xb)
        move(ds.at[k], dxo.at[k], k, DOT_X + 2, to_xo)

    def rs1(k):
        for h in range(2):
            arrived(ra.at[k, h], k, RS_R1 + 3 * h, far_to[h][1])
            rst[k, h] = add(ra[k, h], chip_line(k, h, far_at[h][2])[...]).astype(BF16)
            move(rst.at[k, h], rc.at[k, h], k, RS_R1 + 3 * h + 2, far_to[h][0])

    def rs2(k):
        for h in range(2):
            arrived(rb.at[k, h], k, RS_R1 + 3 * h + 1, far_to[h][0])
            arrived(rc.at[k, h], k, RS_R1 + 3 * h + 2, far_to[h][1])
            rsum[k, h] = add(chip_line(k, h, far_at[h][0])[...], rb[k, h], rc[k, h]).astype(BF16)
            for n, i in enumerate((2, 1, 3)):
                move(rsum.at[k, h, near_at[h][i]], (qa, qb, qc)[n].at[k, h], k, RS_R2 + 3 * h + n, near_to[h][n])
        arrived(dxf.at[k], k, DOT_X, to_xb)
        arrived(dxb.at[k], k, DOT_X + 1, to_xf)
        arrived(dxo.at[k], k, DOT_X + 2, to_xo)
        dr[k] = ds[k] + dxf[k] + dxb[k] + dxo[k]
        move(dr.at[k], dzf.at[k], k, DOT_Z, to_zf)
        move(dr.at[k], dzb.at[k], k, DOT_Z + 1, to_zb)
        move(dr.at[k], dzo.at[k], k, DOT_Z + 2, to_zo)

    def rs4(k):
        arrived(dzf.at[k], k, DOT_Z, to_zb)
        arrived(dzb.at[k], k, DOT_Z + 1, to_zf)
        arrived(dzo.at[k], k, DOT_Z + 2, to_zo)
        dots = (dr[k] + dzf[k] + dzb[k] + dzo[k])[0:1]
        inverse = inv_s[k][0:1]
        pull = dots * inverse * inverse / D
        for h in range(2):
            for n, i in enumerate((1, 0, 2)):
                arrived((qa, qb, qc)[n].at[k, h], k, RS_R2 + 3 * h + n, near_to[h][i])
            norm_grad = add(rsum[k, h, near_at[h][0]], qa[k, h], qb[k, h], qc[k, h])
            span = slice(h * HALF, (h + 1) * HALF)
            cols = slice(k * tok, (k + 1) * tok)
            full = og_own_ref[span, cols].astype(F32) + gain_own_ref[span, 0:1].astype(F32) * inverse * norm_grad
            full = full - res_ref[span, cols].astype(F32) * pull
            out_ref[span, cols] = full.astype(BF16)

    for k in range(CHUNKS):
        ag1(k)
    hidden(0)
    local[0].start()
    local[1].start()
    hidden(1)
    ag3(0)
    ag3(1)
    hidden(2)
    hidden(3)
    hidden(4)
    ag4(0)
    ag3(2)
    hidden(5)
    local[2].start()
    local[3].start()
    hidden(6)
    ag5(0)
    ag4(1)
    hidden(7)
    ag6(0)
    gates(0, 0)
    ag5(1)
    gates(0, 1)
    gates(0, 2)
    ag4(2)
    gates(0, 3)
    last(0, 0)
    last(0, 1)
    last(0, 2)
    ag5(2)
    last(0, 3)
    ag6(1)
    gates(1, 0)
    rs0(0)
    rs0b(0)
    gates(1, 1)
    gates(1, 2)
    gates(1, 3)
    last(1, 0)
    last(1, 1)
    rs1(0)
    last(1, 2)
    last(1, 3)
    ag6(2)
    gates(2, 0)
    rs0(1)
    rs0b(1)
    gates(2, 1)
    rs2(0)
    gates(2, 2)
    gates(2, 3)
    last(2, 0)
    last(2, 1)
    rs1(1)
    last(2, 2)
    last(2, 3)
    rs0(2)
    rs0b(2)
    rs2(1)
    rs4(0)
    rs1(2)
    rs4(1)
    rs2(2)
    rs4(2)
    for copy in sent:
        copy.wait_send()


def core(residual, out_grad_t, gain_own, og_ext, w_down, w_gate, w_up, w_gate_t, w_up_t):
    width = residual.shape[1]
    tok = width // CHUNKS
    hid = w_gate.shape[1]
    vm = pl.BlockSpec(memory_space=pltpu.VMEM)
    hbm = pl.BlockSpec(memory_space=pl.ANY)

    def bf(*shape):
        return pltpu.VMEM(shape, BF16)

    def fl(*shape):
        return pltpu.VMEM(shape, F32)

    rows = SIDE * 2 * 2 * HALF
    return pl.pallas_call(
        core_kernel,
        out_shape=jax.ShapeDtypeStruct(residual.shape, BF16),
        in_specs=[vm] * 3 + [hbm] * 6,
        out_specs=vm,
        scratch_shapes=[
            bf(CHUNKS, SIDE, SIDE, 2, 2, HALF, tok),
            bf(D, 2 * hid), bf(2 * hid, D),
            bf(D, 128),
            bf(2, KB, width), bf(2, hid, KB),
            fl(hid, width),
            bf(rows, tok), fl(2 * hid, tok), fl(8, tok), bf(2 * hid, tok), fl(CHUNKS, 8, tok),
            bf(CHUNKS, SIDE, SIDE, 2, 2, HALF, tok), bf(CHUNKS, SIDE, SIDE, 2, HALF, tok),
        ]
        + [bf(CHUNKS, 2, SIDE, HALF, tok)] * 5
        + [bf(CHUNKS, 2, HALF, tok)] * 3
        + [fl(CHUNKS, 8, tok)] * 10
        + [
            pltpu.SemaphoreType.DMA((CHUNKS, SLOTS)),
            pltpu.SemaphoreType.DMA((CHUNKS, SLOTS)),
            pltpu.SemaphoreType.DMA((5,)),
            pltpu.SemaphoreType.DMA((2, 2)),
        ],
        compiler_params=pltpu.CompilerParams(
            collective_id=0, has_side_effects=True, vmem_limit_bytes=60 * 1024 * 1024
        ),
        cost_estimate=pl.CostEstimate(flops=10 * D * hid * width, bytes_accessed=40_000_000, transcendentals=0),
        name="core",
    )(residual, out_grad_t, gain_own, og_ext, w_down, w_gate, w_up, w_gate_t, w_up_t)


MESH = pl.DeviceIdType.MESH
SLOT = 32
SPANS = ((0, 512), (512, 384))


def nt(a, b):
    return lax.dot_general(a, b, (((1,), (1,)), ((), ())), preferred_element_type=F32)


def fetch_kernel(
    tok_ref, og_ref, ten_ref, halves_ref, table_hbm, wg_hbm, wu_hbm,
    res_ref, og_out, wanted_ref, place_ref, wgt_hbm, wut_hbm,
    tbuf, earlier, rows_s, rows_r, turned, landed, acc, w_buf, wt_buf, table_ref,
    tsend, trecv, ysend, yrecv, psend, precv, gsend, grecv, lsem,
):
    d = lax.axis_index("dp")
    t = lax.axis_index("tensor")
    me = d * 32 + t
    x = t // 8
    z = lax.rem(t // 2, 4)
    c = lax.rem(t, 2)
    step = 1 - 2 * c
    xf, xb, xo = lax.rem(x + step + 4, 4), lax.rem(x - step + 4, 4), lax.rem(x + 2, 4)
    zf, zb, zo = lax.rem(z + step + 4, 4), lax.rem(z - step + 4, 4), lax.rem(z + 2, 4)

    def dev(xx, zz, cc):
        return {"dp": d, "tensor": (xx * 4 + zz) * 2 + cc}

    to_xf, to_xb = dev(xf, z, c), dev(xb, z, c)
    to_zf, to_zb = dev(x, zf, c), dev(x, zb, c)
    to_xo, to_zo = dev(xo, z, c), dev(x, zo, c)
    to_sib = dev(x, z, 1 - c)
    width = tok_ref.shape[1]
    feat = tok_ref.shape[0]
    parts = D // feat

    own_copies = [
        pltpu.make_async_copy(og_ref.at[pl.ds(h * HALF, HALF)], og_out.at[x, z, c, h], lsem.at[h]) for h in range(2)
    ]
    for copy in own_copies:
        copy.start()
    w_in = [pltpu.make_async_copy(src, w_buf.at[n], lsem.at[2 + n]) for n, src in enumerate((wg_hbm, wu_hbm))]
    w_out = [pltpu.make_async_copy(wt_buf.at[n], dst, lsem.at[4 + n]) for n, dst in enumerate((wgt_hbm, wut_hbm))]
    table_in = pltpu.make_async_copy(table_hbm, table_ref, lsem.at[6])
    table_in.start()
    for copy in w_in:
        copy.start()
    barrier = pltpu.get_barrier_semaphore()

    def greet(o, carry):
        pl.semaphore_signal(
            barrier, inc=1, device_id={"dp": d, "tensor": lax.rem(t + o, parts)}, device_id_type=MESH
        )
        return carry

    lax.fori_loop(1, parts, greet, 0)
    for o in (1, 2, 3):
        pl.semaphore_signal(barrier, inc=1, device_id={"dp": lax.rem(d + o, 4), "tensor": t}, device_id_type=MESH)
    pl.semaphore_wait(barrier, parts - 1 + 3)

    sent = []

    def send(src, dst, ssem, rsem, where):
        copy = pltpu.make_async_remote_copy(
            src_ref=src, dst_ref=dst, send_sem=ssem, recv_sem=rsem, device_id=where, device_id_type=MESH
        )
        copy.start()
        sent.append(copy)

    def got(dst, ssem, rsem, where):
        pltpu.make_async_remote_copy(
            src_ref=dst, dst_ref=dst, send_sem=ssem, recv_sem=rsem, device_id=where, device_id_type=MESH
        ).wait_recv()

    for o in (1, 3, 2):
        there = lax.rem(d + o, 4)
        send(ten_ref, tbuf.at[d], tsend.at[there], trecv.at[d], {"dp": there, "tensor": t})

    near_to = ((to_zf, to_zb, to_zo), (to_xf, to_xb, to_xo))
    far_to = ((to_xf, to_xb), (to_zf, to_zb))
    near_at = ((z, zb, zf, zo), (x, xb, xf, xo))
    far_at = ((x, xb, xf, xo), (z, zb, zf, zo))

    def lanes(k):
        return pl.ds(SPANS[k][0], SPANS[k][1])

    def near(k, h, at):
        return og_out.at[x, at, c, 0, :, lanes(k)] if h == 0 else og_out.at[at, z, c, 1, :, lanes(k)]

    def line(k, h, at, cc):
        return og_out.at[at, :, cc, 0, :, lanes(k)] if h == 0 else og_out.at[:, at, cc, 1, :, lanes(k)]

    def move(src, dst, k, slot, where):
        send(src, dst, gsend.at[k, slot], grecv.at[k, slot], where)

    def arrived(dst, k, slot, where):
        got(dst, gsend.at[k, slot], grecv.at[k, slot], where)

    def ag1(k):
        for h in range(2):
            own = near(k, h, near_at[h][0])
            src = og_ref.at[pl.ds(h * HALF, HALF), lanes(k)]
            for n in range(3):
                move(src, own, k, AG_P1 + 3 * h + n, near_to[h][n])

    def ag3(k):
        for h in range(2):
            for n, i in enumerate((1, 0, 2)):
                arrived(near(k, h, near_at[h][n + 1]), k, AG_P1 + 3 * h + n, near_to[h][i])
            own = line(k, h, far_at[h][0], c)
            move(own, own, k, AG_P2 + 3 * h, far_to[h][0])
            move(own, own, k, AG_P2 + 3 * h + 1, far_to[h][1])
            move(own, own, k, AG_SIB + 4 * h, to_sib)

    def ag4(k):
        for h in range(2):
            behind = line(k, h, far_at[h][1], c)
            arrived(behind, k, AG_P2 + 3 * h, far_to[h][1])
            move(behind, behind, k, AG_P2 + 3 * h + 2, far_to[h][0])
            move(behind, behind, k, AG_SIB + 4 * h + 1, to_sib)
        for h in range(2):
            ahead = line(k, h, far_at[h][2], c)
            arrived(ahead, k, AG_P2 + 3 * h + 1, far_to[h][0])
            move(ahead, ahead, k, AG_SIB + 4 * h + 2, to_sib)

    def ag5(k):
        for h in range(2):
            opposite = line(k, h, far_at[h][3], c)
            arrived(opposite, k, AG_P2 + 3 * h + 2, far_to[h][1])
            move(opposite, opposite, k, AG_SIB + 4 * h + 3, to_sib)

    def ag6(k):
        for h in range(2):
            for n, i in enumerate((0, 2, 1, 3)):
                arrived(line(k, h, far_at[h][i], 1 - c), k, AG_SIB + 4 * h + n, to_sib)

    ag1(0)
    ag1(1)

    lines = halves_ref.shape[1]
    earlier[...] = (
        lax.broadcasted_iota(jnp.int32, (width, width), 0) < lax.broadcasted_iota(jnp.int32, (width, width), 1)
    ).astype(F32).astype(BF16)

    def hot(index, size):
        return (lax.broadcasted_iota(jnp.int32, (size, width), 0) == index).astype(F32)

    def look_up(tenant):
        picked = jnp.dot(halves_ref[...], hot(tenant // 128, lines).astype(BF16), preferred_element_type=F32)
        lane = hot(lax.rem(tenant, 128), 128)
        owner = jnp.sum(lane * picked[:128], axis=0, keepdims=True).astype(jnp.int32)
        row = jnp.sum(lane * picked[128:], axis=0, keepdims=True).astype(jnp.int32)
        return owner, row

    def ranks(matches):
        before = jnp.dot(matches.astype(BF16), earlier[...], preferred_element_type=F32)
        return jnp.sum(matches * before, axis=0, keepdims=True).astype(jnp.int32)

    owner, row = look_up(ten_ref[0:1])
    rank = ranks(hot(owner, 128))
    place = lax.rem(owner, 32) * 128 + owner // 32 * SLOT + rank
    place_ref[...] = jnp.broadcast_to(place, place_ref.shape)

    tbuf[d] = ten_ref[...]
    for o in (1, 3, 2):
        there = lax.rem(d + o, 4)
        got(tbuf.at[there], tsend.at[there], trecv.at[there], {"dp": there, "tensor": t})
    for g in range(4):
        owner, row = look_up(tbuf[g, 0:1])
        mine = (owner == me).astype(F32)
        mine8 = jnp.broadcast_to(mine, (8, width))
        before = jnp.dot(mine8.astype(BF16), earlier[...], preferred_element_type=F32)[0:1]
        slot = jnp.where(mine > 0, before.astype(jnp.int32), -1)
        wanted = nt(hot(slot, SLOT).astype(BF16), hot(row, table_ref.shape[0]).astype(BF16)).astype(BF16)
        wanted_ref[g * SLOT:(g + 1) * SLOT] = wanted

    quarter = D // 4

    def y_copy(q, there, at):
        return pltpu.make_async_remote_copy(
            src_ref=rows_s.at[q, there], dst_ref=rows_r.at[q, at], send_sem=ysend.at[q, there], recv_sem=yrecv.at[q, at],
            device_id={"dp": there, "tensor": t}, device_id_type=MESH,
        )

    others = tuple(lax.rem(d + o, 4) for o in (1, 3, 2))
    order = (x, lax.rem(x + 1, 4), lax.rem(x + 3, 4), xo)

    def pick(q):
        cols = pl.ds(pl.multiple_of(q * quarter, quarter), quarter)
        picked = jnp.dot(wanted_ref[...], table_ref[:, cols], preferred_element_type=F32)
        rows_s[q] = picked.astype(BF16).reshape(4, SLOT, quarter)
        for there in others:
            y_copy(q, there, d).start()
        rows_r[q, d] = rows_s[q, d]

    table_in.wait()
    for q in order:
        pick(q)
    for copy in own_copies:
        copy.wait()
    ag3(0)
    ag3(1)

    def turn_weight(n):
        w_in[n].wait()
        wide = 640

        def body(i, carry):
            at = pl.multiple_of(i * wide, wide)
            wt_buf[n, :, pl.ds(at, wide)] = w_buf[n, pl.ds(at, wide), :].T
            return carry

        lax.fori_loop(0, D // wide, body, 0)
        w_out[n].start()

    def plane_copy(there):
        return pltpu.make_async_remote_copy(
            src_ref=turned.at[there], dst_ref=landed.at[t], send_sem=psend.at[there], recv_sem=precv.at[t],
            device_id={"dp": d, "tensor": there}, device_id_type=MESH,
        )

    row = parts // 4

    def pass_on(n):
        q = order[n]
        for there in others:
            pltpu.make_async_remote_copy(
                src_ref=rows_r.at[q, there], dst_ref=rows_r.at[q, there],
                send_sem=ysend.at[q, there], recv_sem=yrecv.at[q, there],
                device_id={"dp": there, "tensor": t}, device_id_type=MESH,
            ).wait_recv()
        turned[pl.ds(q * row, row)] = rows_r[q].reshape(4 * SLOT, quarter).T.reshape(row, feat, 4 * SLOT)

        def scatter(i, carry):
            plane_copy(q * row + lax.rem(lax.rem(t, row) + i, row)).start()
            return carry

        lax.fori_loop(1 if n == 0 else 0, row, scatter, 0)
        if n == 0:
            landed[t] = turned[t]

    pass_on(0)
    pass_on(1)
    pass_on(2)
    ag4(0)
    pass_on(3)
    turn_weight(0)
    acc[...] = tok_ref[...].astype(F32)
    ag4(1)
    turn_weight(1)
    ag5(0)

    def arrive(src):
        @pl.when(src != t)
        def _():
            pltpu.make_async_remote_copy(
                src_ref=landed.at[src], dst_ref=landed.at[src], send_sem=psend.at[src], recv_sem=precv.at[src],
                device_id={"dp": d, "tensor": src}, device_id_type=MESH,
            ).wait_recv()

    def gather(q):
        def body(i, carry):
            pair = q * (row // 2) + i
            arrive(2 * pair)
            arrive(2 * pair + 1)
            sel = (lax.broadcasted_iota(jnp.int32, (256, width), 0) + pair * 256 == place).astype(F32).astype(BF16)
            both = jnp.concatenate([landed[2 * pair], landed[2 * pair + 1]], axis=1)
            acc[...] += jnp.dot(both, sel, preferred_element_type=F32)
            return carry

        lax.fori_loop(0, row // 2, body, 0)

    gather(x)
    ag5(1)
    gather(order[2])
    gather(order[1])
    ag6(0)
    gather(xo)
    res_ref[...] = acc[...].astype(BF16)
    ag6(1)

    def drain(o, carry):
        plane_copy(lax.rem(t + o, parts)).wait_send()
        return carry

    lax.fori_loop(1, parts, drain, 0)
    for q in range(4):
        for there in others:
            y_copy(q, there, d).wait_send()
    for copy in sent:
        copy.wait_send()
    for copy in w_out:
        copy.wait()


def fetch(tokens_t, og_ext, tenant8, halves, table, w_gate, w_up):
    feat, width = tokens_t.shape
    parts = D // feat
    vm = pl.BlockSpec(memory_space=pltpu.VMEM)
    hbm = pl.BlockSpec(memory_space=pl.ANY)
    dma = pltpu.SemaphoreType.DMA
    return pl.pallas_call(
        fetch_kernel,
        out_shape=(
            jax.ShapeDtypeStruct((feat, width), BF16),
            jax.ShapeDtypeStruct((SIDE, SIDE, 2, 2, HALF, og_ext.shape[1]), BF16),
            jax.ShapeDtypeStruct((4 * SLOT, table.shape[0]), BF16),
            jax.ShapeDtypeStruct((8, width), jnp.int32),
            jax.ShapeDtypeStruct(w_gate.shape[::-1], BF16),
            jax.ShapeDtypeStruct(w_up.shape[::-1], BF16),
        ),
        in_specs=[vm] * 4 + [hbm] * 3,
        out_specs=(vm, hbm, vm, vm, hbm, hbm),
        scratch_shapes=[
            pltpu.VMEM((4, 8, width), jnp.int32),
            pltpu.VMEM((width, width), BF16),
            pltpu.VMEM((4, 4, SLOT, D // 4), BF16),
            pltpu.VMEM((4, 4, SLOT, D // 4), BF16),
            pltpu.VMEM((parts, feat, 4 * SLOT), BF16),
            pltpu.VMEM((parts, feat, 4 * SLOT), BF16),
            pltpu.VMEM((feat, width), F32),
            pltpu.VMEM((2,) + w_gate.shape, BF16),
            pltpu.VMEM((2,) + w_gate.shape[::-1], BF16),
            pltpu.VMEM(table.shape, BF16),
            dma((4,)), dma((4,)), dma((4, 4)), dma((4, 4)), dma((parts,)), dma((parts,)),
            dma((len(SPANS), RS_SIB)), dma((len(SPANS), RS_SIB)), dma((7,)),
        ],
        compiler_params=pltpu.CompilerParams(
            collective_id=1, has_side_effects=True, vmem_limit_bytes=62 * 1024 * 1024
        ),
        cost_estimate=pl.CostEstimate(flops=4_000_000_000, bytes_accessed=20_000_000, transcendentals=0),
        name="fetch",
    )(tokens_t, og_ext, tenant8, halves, table, w_gate, w_up)


def give_kernel(full_ref, place_ref, rows_r, leaving, landed, rows_s, psend, precv, ysend, yrecv):
    d = lax.axis_index("dp")
    t = lax.axis_index("tensor")
    feat, width = full_ref.shape
    parts = D // feat
    barrier = pltpu.get_barrier_semaphore()

    def greet(o, carry):
        pl.semaphore_signal(
            barrier, inc=1, device_id={"dp": d, "tensor": lax.rem(t + o, parts)}, device_id_type=MESH
        )
        return carry

    lax.fori_loop(1, parts, greet, 0)
    for o in (1, 2, 3):
        pl.semaphore_signal(barrier, inc=1, device_id={"dp": lax.rem(d + o, 4), "tensor": t}, device_id_type=MESH)

    place = place_ref[0:1]
    pl.semaphore_wait(barrier, parts - 1 + 3)

    def plane_copy(there, at):
        return pltpu.make_async_remote_copy(
            src_ref=leaving.at[there], dst_ref=landed.at[at], send_sem=psend.at[there], recv_sem=precv.at[at],
            device_id={"dp": d, "tensor": there}, device_id_type=MESH,
        )

    def pack(pair):
        sel = (lax.broadcasted_iota(jnp.int32, (256, width), 0) + pair * 256 == place).astype(F32).astype(BF16)
        packed = nt(full_ref[...], sel).astype(BF16)
        for half in range(2):
            there = 2 * pair + half
            leaving[there] = packed[:, 128 * half:128 * half + 128]

            @pl.when(there != t)
            def _():
                plane_copy(there, t).start()

    quad = parts // 8
    x = t // 8

    def own_row(i, carry):
        pack(x * quad + lax.rem(lax.rem(t // 2, quad) + i, quad))
        return carry

    def side_rows(i, carry):
        at = lax.rem(lax.rem(t // 2, quad) + i, quad)
        pack(lax.rem(x + 1, 4) * quad + at)
        pack(lax.rem(x + 3, 4) * quad + at)
        return carry

    def far_row(i, carry):
        pack(lax.rem(x + 2, 4) * quad + lax.rem(lax.rem(t // 2, quad) + i, quad))
        return carry

    lax.fori_loop(0, quad, own_row, 0)
    landed[t] = leaving[t]
    lax.fori_loop(0, quad, side_rows, 0)
    lax.fori_loop(0, quad, far_row, 0)

    group = 8

    def y_copy(q, there):
        return pltpu.make_async_remote_copy(
            src_ref=rows_s.at[q, there], dst_ref=rows_r.at[q, d], send_sem=ysend.at[q, there], recv_sem=yrecv.at[q, d],
            device_id={"dp": there, "tensor": t}, device_id_type=MESH,
        )

    def arrive(src):
        @pl.when(src != t)
        def _():
            pltpu.make_async_remote_copy(
                src_ref=landed.at[src], dst_ref=landed.at[src], send_sem=psend.at[src], recv_sem=precv.at[src],
                device_id={"dp": d, "tensor": src}, device_id_type=MESH,
            ).wait_recv()

    for q in (x, lax.rem(x + 3, 4), lax.rem(x + 1, 4), lax.rem(x + 2, 4)):

        def take(i, inner):
            arrive(q * group + i)
            return inner

        lax.fori_loop(0, group, take, 0)
        block = landed[pl.ds(q * group, group)].reshape(group * feat, 4 * SLOT)
        rows_s[q] = block.T.reshape(4, SLOT, group * feat)
        for o in (1, 3, 2):
            y_copy(q, lax.rem(d + o, 4)).start()
        rows_r[q, d] = rows_s[q, d]

    def finish(q, carry):
        for o in (1, 3, 2):
            there = lax.rem(d + o, 4)
            y_copy(q, there).wait_send()
            pltpu.make_async_remote_copy(
                src_ref=rows_r.at[q, there], dst_ref=rows_r.at[q, there],
                send_sem=ysend.at[q, there], recv_sem=yrecv.at[q, there],
                device_id={"dp": there, "tensor": t}, device_id_type=MESH,
            ).wait_recv()
        return carry

    lax.fori_loop(0, 4, finish, 0)

    def drain(o, carry):
        plane_copy(lax.rem(t + o, parts), t).wait_send()
        return carry

    lax.fori_loop(1, parts, drain, 0)


def give(full_grad, place):
    feat, width = full_grad.shape
    parts = D // feat
    vm = pl.BlockSpec(memory_space=pltpu.VMEM)
    dma = pltpu.SemaphoreType.DMA
    return pl.pallas_call(
        give_kernel,
        out_shape=jax.ShapeDtypeStruct((4, 4, SLOT, D // 4), BF16),
        in_specs=[vm] * 2,
        out_specs=vm,
        scratch_shapes=[
            pltpu.VMEM((parts, feat, 4 * SLOT), BF16),
            pltpu.VMEM((parts, feat, 4 * SLOT), BF16),
            pltpu.VMEM((4, 4, SLOT, D // 4), BF16),
            dma((parts,)), dma((parts,)), dma((4, 4)), dma((4, 4)),
        ],
        compiler_params=pltpu.CompilerParams(
            collective_id=2, has_side_effects=True, vmem_limit_bytes=48 * 1024 * 1024
        ),
        cost_estimate=pl.CostEstimate(flops=2_000_000_000, bytes_accessed=3_000_000, transcendentals=0),
        name="give",
    )(full_grad, place)


def per_device(tokens_in, out_grad, tenant, slot_of, steer_table, norm_gain, w_gate, w_up, w_down):
    feat_local = tokens_in.shape[1]
    token_count = tenant.shape[0]
    out_grad_t = out_grad.T
    gain_own = jnp.broadcast_to(norm_gain[:, None], (feat_local, 128))
    lines = slot_of.reshape(-1, 128).T
    halves = jnp.concatenate([lines // 256, lines % 256], axis=0).astype(BF16)
    tenant8 = jnp.broadcast_to(tenant[None, :], (8, token_count))
    residual, og_ext, wanted, place, w_gate_t, w_up_t = fetch(
        tokens_in.T, jnp.concatenate([out_grad_t, gain_own], axis=1), tenant8, halves, steer_table, w_gate, w_up
    )
    og_ext = og_ext.reshape(D, token_count + 128)
    full_grad = core(residual, out_grad_t, gain_own, og_ext, w_down, w_gate, w_up, w_gate_t, w_up_t)
    rows = give(full_grad, place)
    rows = rows.transpose(1, 2, 0, 3).reshape(4 * SLOT, D)
    table_grad = lax.dot_general(wanted, rows, (((0,), (0,)), ((), ())), preferred_element_type=F32)
    return (full_grad.T, table_grad)


def solution(mesh):
    placed = (
        P("dp", "tensor"),
        P("dp", "tensor"),
        P("dp"),
        P(),
        P(("dp", "tensor"), None),
        P("tensor"),
        P(None, "tensor"),
        P(None, "tensor"),
        P("tensor", None),
    )
    return jax.shard_map(
        per_device,
        mesh=mesh,
        in_specs=placed,
        out_specs=(P("dp", "tensor"), P(("dp", "tensor"), None)),
        check_vma=False,
    )
```
